256 devices in a mesh: dp: 128 (over y, z, x), layer: 2 (over core).
Axes of the slice: x: 4, y: 4, z: 8, core: 2. Of those that a mesh axis runs over, the one named last changes fastest.
Arguments:
- activations: bfloat16 [2, 65536, 4608], P('layer', 'dp'), may hold values from -6 to 6
- out_grads: bfloat16 [2, 65536, 4096], P('layer', 'dp'), may hold values from -6 to 6
- proj_in: bfloat16 [2, 4608, 64], P('layer'), may hold values from -0.09375 to 0.09375
- proj_out: bfloat16 [2, 4096, 64], P('layer'), may hold values from -0.09375 to 0.09375
- precond_out: float32 [2, 64, 64], P('layer'), may hold values from -0.75 to 0.75
- precond_in: float32 [2, 64, 64], P('layer'), may hold values from -0.75 to 0.75
- step_lengths: int32 [128, 32], P('dp'), may hold values from 1 to 64, 512 in all within a row
- flagged_owner: int32 [4], replicated, may hold values from 0 to 127
- flagged_step: int32 [4], replicated, may hold values from 0 to 31
- retrieval: int32 [4, 4096], P(None, 'dp'), may hold values from 0 to 4095, as said below
Outputs:
- scores: float32 [4, 4096], P(None, 'dp')
The draws below stay inside these ranges and needn't reach their ends.
Inputs may be any that keep to these rules, and one draw needn't show every extreme that they name: `retrieval`: an id c names step c % 32 of shard c // 32. Among the 128 ids of one dp shard's columns, at most 2 are stored on any one shard, and every shard named there is named exactly 2 times.
All inputs are finite; a program needn't handle non-finite values.
Results may differ from the reference program's by a relative error of at most 0.0076.
Values may be sent and summed in bfloat16 or wider, within the bound.
No kernel may reach another device: no remote copies, remote signals or barrier semaphores. Data moves between devices by JAX's collectives and lax.ppermute only.
A program may use at most 64 MiB of HBM per device.

```python
import math
import jax
import jax.numpy as jnp
import numpy as np
from jax import lax

D = 4608
Q = 4096
R = 64
TOK_DEV = 512
NQ = 4
K_DEV = 32
STEPS_DEV = 32
STEP_MAX = 64
LAYERS = 2
SHARDS = 128
TOKENS = 65536
CAP = 2


def draw_retrieval(key, part):
    key = jax.random.fold_in(key, 7)
    request_count = NQ * K_DEV
    groups = request_count // CAP

    def per_scorer(scorer_key):
        key_a, key_b, key_c = jax.random.split(scorer_key, 3)
        position = jax.random.permutation(key_a, request_count)
        sources = jax.random.permutation(key_b, SHARDS)[:groups]
        source = sources[position // CAP]
        local_step = jax.random.randint(key_c, (request_count,), 0, STEPS_DEV)
        return (source * STEPS_DEV + local_step).astype(jnp.int32)
    table = jax.vmap(per_scorer)(jax.random.split(key, SHARDS))
    return table.reshape(SHARDS, NQ, K_DEV).transpose(1, 0, 2).reshape(NQ, SHARDS * K_DEV)


def with_ends(array, own_key, smallest, largest):
    dims = array.shape
    spot = [jax.random.randint(jax.random.fold_in(own_key, axis), (), 0, dims[axis]) for axis in range(len(dims))]
    array = array.at[tuple(spot)].set(smallest)
    longest = dims.index(max(dims))
    spot[longest] = (spot[longest] + 1) % dims[longest]
    return array.at[tuple(spot)].set(largest)


def steps_of(key, dims, cuts, least, largest):
    def one(dim, blocks):
        draws = jax.random.uniform(jax.random.fold_in(jax.random.fold_in(key, 6), dim), (blocks,), jnp.float32, least / len(cuts), largest / len(cuts))
        return jnp.repeat(jnp.exp(draws), dims[dim] // blocks).reshape((-1,) + (1,) * (len(dims) - dim - 1))

    loudness = one(*cuts[0])
    for cut in cuts[1:]:
        loudness = loudness * one(*cut)
    return loudness


def length_profile(number_of, total, reach, slope):
    loads = [(1 << 20) // math.isqrt(rank ** slope) + 1 for rank in range(2, number_of + 1)]
    surplus, holding = total - reach - (number_of - 1), [1] * (number_of - 1)
    while surplus > 0:
        movable = [i for i in range(number_of - 1) if holding[i] < reach]
        whole, budget = sum([loads[i] for i in movable]), surplus
        for i in movable:
            extra = min(reach - holding[i], max(1, budget * loads[i] // whole), surplus)
            holding[i] = holding[i] + extra
            surplus = surplus - extra
    return np.array([reach] + holding)


def ragged_sizes(stream_key, count, total, bound, slope):
    if count == 2:
        one = jax.random.randint(stream_key, (), max(1, total - bound), min(bound, total - 1) + 1)
        return jnp.stack([one, total - one])
    lengths = jnp.asarray(length_profile(count, total, bound, slope), jnp.int32)
    couples = (count - 1) // 2
    donor, receiver = lengths[1:1 + 2 * couples:2], lengths[2:2 + 2 * couples:2]
    room = jnp.minimum(donor - 1, bound - receiver)
    moved = jax.random.randint(jax.random.fold_in(stream_key, 1), (couples,), 0, 1 << 20) % (room + 1)
    lengths = lengths.at[1:1 + 2 * couples:2].set(donor - moved).at[2:2 + 2 * couples:2].set(receiver + moved)
    return lengths[jax.random.permutation(jax.random.fold_in(stream_key, 2), count)]


def noise(key, shape, scale, limit, pieces=(), kind=jnp.bfloat16):
    result = scale * jax.random.normal(key, shape, jnp.float32)
    if pieces:
        result = result * steps_of(key, shape, pieces, -0.22, 0.18)
    return jnp.clip(result, -limit, limit).astype(kind)


def setup_inputs(seed: int = 0) -> dict:
    streams_of = jax.random.split(jax.random.key(seed), 11)
    return {
        "activations": noise(streams_of[0], (LAYERS, TOKENS, D), 1.0, 6.0, ((0, 2), (1, 128))),
        "out_grads": noise(streams_of[1], (LAYERS, TOKENS, Q), 1.0, 6.0, ((0, 2), (1, 128))),
        "proj_in": noise(streams_of[2], (LAYERS, D, R), D ** -0.5, 0.09375, ((0, 2),)),
        "proj_out": noise(streams_of[3], (LAYERS, Q, R), Q ** -0.5, 0.09375, ((0, 2),)),
        "precond_out": noise(streams_of[4], (LAYERS, R, R), R ** -0.5, 0.75, ((0, 2),), jnp.float32),
        "precond_in": noise(streams_of[5], (LAYERS, R, R), R ** -0.5, 0.75, ((0, 2),), jnp.float32),
        "step_lengths": jax.vmap(lambda own: ragged_sizes(own, STEPS_DEV, TOK_DEV, STEP_MAX, 1))(jax.random.split(streams_of[6], SHARDS)).reshape((SHARDS, STEPS_DEV)).astype(jnp.int32),
        "flagged_owner": with_ends(jax.random.randint(streams_of[7], (NQ,), 0, SHARDS), jax.random.fold_in(streams_of[7], 1), 0, SHARDS - 1).astype(jnp.int32),
        "flagged_step": with_ends(jax.random.randint(streams_of[8], (NQ,), 0, STEPS_DEV), jax.random.fold_in(streams_of[8], 1), 0, STEPS_DEV - 1).astype(jnp.int32),
        "retrieval": draw_retrieval(jax.random.fold_in(streams_of[10], 71), 0),
    }


def step_gradients(act_rows, grad_rows, proj_in, proj_out, lengths_row):
    tokens_here = act_rows.shape[1]
    step_count = lengths_row.shape[0]
    low_rank = proj_in.shape[2]
    step_ends = jnp.cumsum(lengths_row).astype(jnp.int32)
    position = jnp.arange(tokens_here, dtype=jnp.int32)
    step_index = jnp.sum((position[:, None] >= step_ends[None, :]).astype(jnp.int32), axis=1)
    member = (step_index[:, None] == jnp.arange(step_count, dtype=jnp.int32)[None, :]).astype(jnp.bfloat16)
    per_layer = []
    for layer_pos in range(act_rows.shape[0]):
        act_low = jnp.dot(act_rows[layer_pos], proj_in[layer_pos], preferred_element_type=jnp.float32).astype(jnp.bfloat16)
        grad_low = jnp.dot(grad_rows[layer_pos], proj_out[layer_pos], preferred_element_type=jnp.float32).astype(jnp.bfloat16)
        spread = (member[:, :, None] * grad_low[:, None, :]).reshape(tokens_here, step_count * low_rank)
        outer = lax.dot_general(spread, act_low, (((0,), (0,)), ((), ())), preferred_element_type=jnp.float32)
        per_layer.append(outer.reshape(step_count, low_rank * low_rank).astype(jnp.bfloat16))
    return jnp.stack(per_layer, axis=1)


def precondition(queries, precond_out, precond_in):
    count = queries.shape[0]
    layers_here = queries.shape[1]
    low_rank = precond_in.shape[1]
    matrices = queries.astype(jnp.float32).reshape(count, layers_here, low_rank, low_rank)
    left_side = jnp.einsum("lab,qlbc->qlac", precond_out, matrices, precision=lax.Precision.HIGHEST)
    both_sides = jnp.einsum("qlac,lcd->qlad", left_side, precond_in, precision=lax.Precision.HIGHEST)
    return both_sides.astype(jnp.bfloat16).reshape(count, layers_here * low_rank * low_rank)


def reference(activations, out_grads, proj_in, proj_out, precond_out, precond_in, step_lengths, flagged_owner, flagged_step, retrieval):
    def per_shard(shard_index):
        act_rows = lax.dynamic_slice_in_dim(activations, shard_index * TOK_DEV, TOK_DEV, 1)
        grad_rows = lax.dynamic_slice_in_dim(out_grads, shard_index * TOK_DEV, TOK_DEV, 1)
        return step_gradients(act_rows, grad_rows, proj_in, proj_out, step_lengths[shard_index])

    all_steps = lax.map(per_shard, jnp.arange(SHARDS, dtype=jnp.int32))
    all_steps = all_steps.reshape(SHARDS * STEPS_DEV, LAYERS * R * R)
    flagged_ids = (flagged_owner * STEPS_DEV + flagged_step).astype(jnp.int32)
    queries = all_steps[flagged_ids].reshape(NQ, LAYERS, R * R)
    weighted = precondition(queries, precond_out, precond_in)
    score_table = jnp.dot(all_steps, weighted.T, preferred_element_type=jnp.float32)
    scores = score_table[retrieval, jnp.arange(NQ, dtype=jnp.int32)[:, None]]
    return scores * (1.0 / (R * STEP_MAX))
```

```python
import functools

import jax
import jax.numpy as jnp
from jax import lax
from jax.experimental import pallas as pl
from jax.experimental.pallas import tpu as pltpu
from jax.sharding import PartitionSpec as P

WINDOW = 80
ALIGN = 16
NT = (((1,), (1,)), ((), ()))
TN = (((0,), (0,)), ((), ()))
HIGHEST = lax.Precision.HIGHEST


def rank_of(owner_ref, query):
    rank = jnp.int32(0)
    for other in range(query):
        rank = rank + jnp.where(owner_ref[other] == owner_ref[query], 1, 0).astype(jnp.int32)
    return rank


def pieces(total, count):
    width = total // count
    return [pl.ds(i * width, width) for i in range(count)]


def flagged_kernel(
    slot,
    owner_ref,
    step_ref,
    lengths_ref,
    act_ref,
    grad_ref,
    proj_in_ref,
    proj_out_ref,
    precond_out_ref,
    precond_in_ref,
    out_ref,
    act_rows,
    grad_rows,
    proj_in,
    proj_out,
    sems,
):
    me = lax.axis_index("dp")
    low_rank = proj_in.shape[0]
    half = low_rank // 2
    tokens = act_ref.shape[0]
    mine = jnp.int32(-1)
    for query in range(owner_ref.shape[0]):
        hit = (owner_ref[query] == me) & (rank_of(owner_ref, query) == slot)
        mine = jnp.where(hit, step_ref[query], mine)

    @pl.when(mine < 0)
    def _():
        out_ref[...] = jnp.zeros_like(out_ref)

    @pl.when(mine >= 0)
    def _():
        begin = jnp.int32(0)
        for step in range(lengths_ref.shape[1]):
            begin = begin + jnp.where(step < mine, lengths_ref[0, step], 0)
        end = begin + lengths_ref[0, mine]
        first = jnp.minimum(begin // ALIGN, (tokens - WINDOW) // ALIGN) * ALIGN
        rows = pl.ds(pl.multiple_of(first, ALIGN), WINDOW)
        act_cols = pieces(act_ref.shape[1], 3)
        grad_cols = pieces(grad_ref.shape[1], 2)
        copies = []
        for columns, source, held, weights, held_weights in (
            [(c, act_ref, act_rows, proj_in_ref, proj_in) for c in act_cols]
            + [(c, grad_ref, grad_rows, proj_out_ref, proj_out) for c in grad_cols]
        ):
            pair = (
                pltpu.make_async_copy(
                    weights.at[:, columns], held_weights.at[:, columns], sems.at[2 * len(copies)]
                ),
                pltpu.make_async_copy(
                    source.at[rows, columns], held.at[:, columns], sems.at[2 * len(copies) + 1]
                ),
            )
            for copy in pair:
                copy.start()
            copies.append(pair)
        lows = []
        done = 0
        for columns_list, held, held_weights in (
            (act_cols, act_rows, proj_in),
            (grad_cols, grad_rows, proj_out),
        ):
            total = jnp.zeros((WINDOW, low_rank), jnp.float32)
            for columns in columns_list:
                for copy in copies[done]:
                    copy.wait()
                done += 1
                total = total + lax.dot_general(
                    held[:, columns],
                    held_weights[:, columns],
                    NT,
                    preferred_element_type=jnp.float32,
                )
            lows.append(total)
        position = first + lax.broadcasted_iota(jnp.int32, (WINDOW, low_rank), 0)
        inside = (position >= begin) & (position < end)
        act_low = lows[0].astype(jnp.bfloat16)
        grad_low = jnp.where(inside, lows[1], 0.0).astype(jnp.bfloat16)
        step_grad = lax.dot_general(grad_low, act_low, TN, preferred_element_type=jnp.float32)
        step_grad = step_grad.astype(jnp.bfloat16).astype(jnp.float32)
        left = jnp.dot(
            precond_out_ref[...], step_grad, precision=HIGHEST, preferred_element_type=jnp.float32
        )
        both = jnp.dot(
            left, precond_in_ref[...], precision=HIGHEST, preferred_element_type=jnp.float32
        )
        packed = jnp.concatenate([both[:half], both[half:]], axis=1).astype(jnp.bfloat16)
        out_ref[...] = jnp.broadcast_to(packed[None], out_ref.shape)


def flagged(slot, shard_count, owner, step, lengths, act, grad, proj_in, proj_out, pre_out, pre_in):
    low_rank = proj_in.shape[0]
    smem = pl.BlockSpec(memory_space=pltpu.SMEM)
    vmem = pl.BlockSpec(memory_space=pltpu.VMEM)
    hbm = pl.BlockSpec(memory_space=pl.ANY)
    return pl.pallas_call(
        functools.partial(flagged_kernel, slot),
        out_shape=jax.ShapeDtypeStruct((shard_count, low_rank // 2, 2 * low_rank), jnp.bfloat16),
        in_specs=[smem, smem, smem, hbm, hbm, hbm, hbm, vmem, vmem],
        out_specs=vmem,
        scratch_shapes=[
            pltpu.VMEM((WINDOW, act.shape[1]), jnp.bfloat16),
            pltpu.VMEM((WINDOW, grad.shape[1]), jnp.bfloat16),
            pltpu.VMEM(proj_in.shape, jnp.bfloat16),
            pltpu.VMEM(proj_out.shape, jnp.bfloat16),
            pltpu.SemaphoreType.DMA((10,)),
        ],
        compiler_params=pltpu.CompilerParams(vmem_limit_bytes=16 << 20),
    )(owner, step, lengths, act, grad, proj_in, proj_out, pre_out, pre_in)


def project_kernel(act_ref, grad_ref, proj_in_ref, proj_out_ref, low_ref, act, grad, proj_in, proj_out, sems):
    low_rank = proj_in.shape[0]
    act_cols = pieces(act.shape[1], 6)
    grad_cols = pieces(grad.shape[1], 4)
    copies = []
    for columns, source, held, weights, held_weights in (
        [(c, act_ref, act, proj_in_ref, proj_in) for c in act_cols]
        + [(c, grad_ref, grad, proj_out_ref, proj_out) for c in grad_cols]
    ):
        pair = (
            pltpu.make_async_copy(
                weights.at[:, columns], held_weights.at[:, columns], sems.at[2 * len(copies)]
            ),
            pltpu.make_async_copy(
                source.at[:, columns], held.at[:, columns], sems.at[2 * len(copies) + 1]
            ),
        )
        for copy in pair:
            copy.start()
        copies.append(pair)
    done = 0
    for index, (columns_list, held, held_weights) in enumerate(
        ((act_cols, act, proj_in), (grad_cols, grad, proj_out))
    ):
        total = jnp.zeros((act.shape[0], low_rank), jnp.float32)
        for columns in columns_list:
            for copy in copies[done]:
                copy.wait()
            done += 1
            total = total + lax.dot_general(
                held[:, columns], held_weights[:, columns], NT, preferred_element_type=jnp.float32
            )
        low_ref[:, index * low_rank : (index + 1) * low_rank] = total.astype(jnp.bfloat16)


def project(act, grad, proj_in, proj_out):
    tokens, low_rank = act.shape[0], proj_in.shape[0]
    hbm = pl.BlockSpec(memory_space=pl.ANY)
    size = 2 * (act.size + grad.size + proj_in.size + proj_out.size)
    return pl.pallas_call(
        project_kernel,
        out_shape=jax.ShapeDtypeStruct((tokens, 2 * low_rank), jnp.bfloat16),
        in_specs=[hbm] * 4,
        out_specs=pl.BlockSpec(memory_space=pltpu.VMEM),
        scratch_shapes=[
            pltpu.VMEM(act.shape, jnp.bfloat16),
            pltpu.VMEM(grad.shape, jnp.bfloat16),
            pltpu.VMEM(proj_in.shape, jnp.bfloat16),
            pltpu.VMEM(proj_out.shape, jnp.bfloat16),
            pltpu.SemaphoreType.DMA((20,)),
        ],
        compiler_params=pltpu.CompilerParams(vmem_limit_bytes=24 << 20),
        cost_estimate=pl.CostEstimate(
            flops=2 * low_rank * (act.size + grad.size), bytes_accessed=size, transcendentals=0
        ),
    )(act, grad, proj_in, proj_out)


def score_kernel(owner_ref, lengths_ref, low_ref, received_ref, more_ref, out_ref, held, sems):
    count = owner_ref.shape[0]
    tokens = low_ref.shape[0]
    low_rank = low_ref.shape[1] // 2
    half = low_rank // 2
    steps = lengths_ref.shape[1]
    ranks = [rank_of(owner_ref, query) for query in range(count)]
    for query in range(count):

        @pl.when(ranks[query] == 0)
        def _():
            pltpu.make_async_copy(
                received_ref.at[owner_ref[query]], held.at[query], sems.at[query]
            ).start()

        @pl.when(ranks[query] > 0)
        def _():
            pltpu.make_async_copy(more_ref.at[query], held.at[query], sems.at[query]).start()

    step_of = lax.broadcasted_iota(jnp.int32, (steps, tokens), 0)
    token_of = lax.broadcasted_iota(jnp.int32, (steps, tokens), 1)
    lengths = lengths_ref[...]
    earlier = lax.broadcasted_iota(jnp.int32, (steps, steps), 1) < lax.broadcasted_iota(
        jnp.int32, (steps, steps), 0
    )
    spread = jnp.broadcast_to(lengths, (steps, steps))
    begins = jnp.sum(jnp.where(earlier, spread, 0), axis=1, keepdims=True)
    same = lax.broadcasted_iota(jnp.int32, (steps, steps), 1) == lax.broadcasted_iota(
        jnp.int32, (steps, steps), 0
    )
    ends = begins + jnp.sum(jnp.where(same, spread, 0), axis=1, keepdims=True)
    member = ((token_of >= begins) & (token_of < ends)).astype(jnp.bfloat16)
    act_low = low_ref[:, :low_rank]
    grad_low = low_ref[:, low_rank:]
    act_wide = act_low.astype(jnp.float32)
    sums = []
    for query in range(count):
        pltpu.make_async_copy(received_ref.at[0], held.at[query], sems.at[query]).wait()
        packed = held[query]
        weighted = jnp.concatenate([packed[:, :low_rank], packed[:, low_rank:]], axis=0)
        turned = jnp.dot(grad_low, weighted, preferred_element_type=jnp.float32)
        value = turned * act_wide
        high = value.astype(jnp.bfloat16)
        low = (value - high.astype(jnp.float32)).astype(jnp.bfloat16)
        summed = jnp.dot(member, high, preferred_element_type=jnp.float32) + jnp.dot(
            member, low, preferred_element_type=jnp.float32
        )
        sums.append(jnp.sum(summed, axis=1, keepdims=True))
    column = lax.broadcasted_iota(jnp.int32, (steps, count * steps), 1)
    row = lax.broadcasted_iota(jnp.int32, (steps, count * steps), 0)
    table = jnp.zeros((steps, count * steps), jnp.float32)
    for query in range(count):
        table = jnp.where(column == row + query * steps, sums[query], table)
    out_ref[...] = jnp.broadcast_to(jnp.sum(table, axis=0, keepdims=True), out_ref.shape)


def score(shard_count, owner, lengths, low, received, more):
    count, steps = owner.shape[0], lengths.shape[1]
    smem = pl.BlockSpec(memory_space=pltpu.SMEM)
    vmem = pl.BlockSpec(memory_space=pltpu.VMEM)
    hbm = pl.BlockSpec(memory_space=pl.ANY)
    return pl.pallas_call(
        score_kernel,
        out_shape=jax.ShapeDtypeStruct((shard_count, count * steps), jnp.float32),
        in_specs=[smem, vmem, vmem, hbm, hbm],
        out_specs=vmem,
        scratch_shapes=[
            pltpu.VMEM((count,) + received.shape[1:], received.dtype),
            pltpu.SemaphoreType.DMA((count,)),
        ],
        compiler_params=pltpu.CompilerParams(vmem_limit_bytes=16 << 20),
    )(owner, lengths, low, received, more)


def pick_kernel(scale, retrieval_ref, table_ref, out_ref):
    count, per_scorer = retrieval_ref.shape
    shard_count, width = table_ref.shape
    steps = width // count
    ids = retrieval_ref[...]
    shard_row = lax.broadcasted_iota(jnp.int32, (shard_count, per_scorer), 0)
    step_row = lax.broadcasted_iota(jnp.int32, (width, per_scorer), 0)
    for query in range(count):
        wanted = ids[query : query + 1]
        source = lax.shift_right_logical(wanted, steps.bit_length() - 1)
        entry = lax.bitwise_and(wanted, steps - 1) + query * steps
        chosen = jnp.where(shard_row == source, 1.0, 0.0)
        values = lax.dot_general(
            table_ref[...], chosen, TN, precision=HIGHEST, preferred_element_type=jnp.float32
        )
        out_ref[query : query + 1] = scale * jnp.sum(
            jnp.where(step_row == entry, values, 0.0), axis=0, keepdims=True
        )


def pick(scale, retrieval, table):
    vmem = pl.BlockSpec(memory_space=pltpu.VMEM)
    return pl.pallas_call(
        functools.partial(pick_kernel, scale),
        out_shape=jax.ShapeDtypeStruct(retrieval.shape, jnp.float32),
        in_specs=[vmem, vmem],
        out_specs=vmem,
    )(retrieval, table)


def local(
    activations,
    out_grads,
    proj_in,
    proj_out,
    precond_out,
    precond_in,
    step_lengths,
    flagged_owner,
    flagged_step,
    retrieval,
):
    shard_count = lax.axis_size("dp")
    low_rank = precond_in.shape[1]
    step_max = 64
    count = flagged_owner.shape[0]
    act, grad = activations[0], out_grads[0]
    into, outof = proj_in[0].T, proj_out[0].T

    def spread(slot):
        own = flagged(
            slot, shard_count, flagged_owner, flagged_step, step_lengths,
            act, grad, into, outof, precond_out[0], precond_in[0],
        )
        return lax.all_to_all(own, "dp", split_axis=0, concat_axis=0, tiled=True)

    earlier = jnp.arange(count)[None, :] < jnp.arange(count)[:, None]
    ranks = jnp.sum((earlier & (flagged_owner[:, None] == flagged_owner[None, :])).astype(jnp.int32), axis=1)

    def further_rounds():
        rounds = jnp.stack([spread(slot)[flagged_owner] for slot in range(1, count)])
        return rounds[jnp.maximum(ranks - 1, 0), jnp.arange(count)]

    def no_further():
        return jnp.zeros((count, low_rank // 2, 2 * low_rank), jnp.bfloat16)

    low = project(act, grad, into, outof)
    received = spread(0)
    more = lax.cond(jnp.max(ranks) > 0, further_rounds, no_further)
    table = score(shard_count, flagged_owner, step_lengths, low, received, more)
    tables = lax.all_to_all(table, "dp", split_axis=0, concat_axis=0, tiled=True)
    partial_value = pick(1.0 / (low_rank * step_max), retrieval, tables)
    other = lax.ppermute(partial_value, "layer", [(0, 1), (1, 0)])
    return partial_value + other


def solution(mesh):
    return jax.shard_map(
        local,
        mesh=mesh,
        in_specs=(
            P("layer", "dp", None),
            P("layer", "dp", None),
            P("layer", None, None),
            P("layer", None, None),
            P("layer", None, None),
            P("layer", None, None),
            P("dp", None),
            P(),
            P(),
            P(None, "dp"),
        ),
        out_specs=P(None, "dp"),
        check_vma=False,
    )
```

```python
import functools

import jax
import jax.numpy as jnp
from jax import lax
from jax.experimental import pallas as pl
from jax.experimental.pallas import tpu as pltpu
from jax.sharding import Mesh, PartitionSpec as P

WINDOW = 80
ALIGN = 16
STEP_MAX = 64
SIZES = (4, 8, 4)
DP = ("y", "z", "x")
PLANE = ("y", "x")
NT = (((1,), (1,)), ((), ()))
TN = (((0,), (0,)), ((), ()))
HIGHEST = lax.Precision.HIGHEST
SMEM = pl.BlockSpec(memory_space=pltpu.SMEM)
VMEM = pl.BlockSpec(memory_space=pltpu.VMEM)
HBM = pl.BlockSpec(memory_space=pl.ANY)


def rank_of(owner_ref, query):
    rank = jnp.int32(0)
    for other in range(query):
        rank = rank + jnp.where(owner_ref[other] == owner_ref[query], 1, 0).astype(jnp.int32)
    return rank


def line_of(owner):
    return lax.rem(lax.div(owner, SIZES[2]), SIZES[1])


def plane_of(owner):
    return lax.div(owner, SIZES[1] * SIZES[2]) * SIZES[2] + lax.rem(owner, SIZES[2])


def pieces(total, count):
    width = total // count
    return [pl.ds(i * width, width) for i in range(count)]


def flagged_kernel(
    slot,
    owner_ref,
    step_ref,
    lengths_ref,
    act_ref,
    grad_ref,
    proj_in_ref,
    proj_out_ref,
    precond_out_ref,
    precond_in_ref,
    out_ref,
    again_ref,
    act_rows,
    grad_rows,
    proj_in,
    proj_out,
    sems,
):
    me = lax.axis_index(DP)
    low_rank = proj_in.shape[0]
    half = low_rank // 2
    tokens = act_ref.shape[0]
    mine = jnp.int32(-1)
    again = jnp.int32(0)
    for query in range(owner_ref.shape[0]):
        rank = rank_of(owner_ref, query)
        again = jnp.maximum(again, rank)
        mine = jnp.where((owner_ref[query] == me) & (rank == slot), step_ref[query], mine)
    again_ref[0] = again

    @pl.when(mine < 0)
    def _():
        out_ref[...] = jnp.zeros_like(out_ref)

    @pl.when(mine >= 0)
    def _():
        begin = jnp.int32(0)
        for step in range(lengths_ref.shape[1]):
            begin = begin + jnp.where(step < mine, lengths_ref[0, step], 0)
        end = begin + lengths_ref[0, mine]
        first = jnp.minimum(begin // ALIGN, (tokens - WINDOW) // ALIGN) * ALIGN
        rows = pl.ds(pl.multiple_of(first, ALIGN), WINDOW)
        act_cols = pieces(act_ref.shape[1], 3)
        grad_cols = pieces(grad_ref.shape[1], 2)
        copies = []
        for columns, source, held, weights, held_weights in (
            [(c, act_ref, act_rows, proj_in_ref, proj_in) for c in act_cols]
            + [(c, grad_ref, grad_rows, proj_out_ref, proj_out) for c in grad_cols]
        ):
            pair = (
                pltpu.make_async_copy(
                    weights.at[:, columns], held_weights.at[:, columns], sems.at[2 * len(copies)]
                ),
                pltpu.make_async_copy(
                    source.at[rows, columns], held.at[:, columns], sems.at[2 * len(copies) + 1]
                ),
            )
            for copy in pair:
                copy.start()
            copies.append(pair)
        lows = []
        done = 0
        for columns_list, held, held_weights in (
            (act_cols, act_rows, proj_in),
            (grad_cols, grad_rows, proj_out),
        ):
            total = jnp.zeros((WINDOW, low_rank), jnp.float32)
            for columns in columns_list:
                for copy in copies[done]:
                    copy.wait()
                done += 1
                total = total + lax.dot_general(
                    held[:, columns],
                    held_weights[:, columns],
                    NT,
                    preferred_element_type=jnp.float32,
                )
            lows.append(total)
        position = first + lax.broadcasted_iota(jnp.int32, (WINDOW, low_rank), 0)
        inside = (position >= begin) & (position < end)
        act_low = lows[0].astype(jnp.bfloat16)
        grad_low = jnp.where(inside, lows[1], 0.0).astype(jnp.bfloat16)
        step_grad = lax.dot_general(grad_low, act_low, TN, preferred_element_type=jnp.float32)
        step_grad = step_grad.astype(jnp.bfloat16).astype(jnp.float32)
        left = jnp.dot(
            precond_out_ref[...], step_grad, precision=HIGHEST, preferred_element_type=jnp.float32
        )
        both = jnp.dot(
            left, precond_in_ref[...], precision=HIGHEST, preferred_element_type=jnp.float32
        )
        packed = jnp.concatenate([both[:half], both[half:]], axis=1).astype(jnp.bfloat16)
        out_ref[...] = jnp.broadcast_to(packed[None], out_ref.shape)


def flagged(slot, peers, owner, step, lengths, act, grad, proj_in, proj_out, pre_out, pre_in):
    low_rank = proj_in.shape[0]
    return pl.pallas_call(
        functools.partial(flagged_kernel, slot),
        out_shape=(
            jax.ShapeDtypeStruct((peers, low_rank // 2, 2 * low_rank), jnp.bfloat16),
            jax.ShapeDtypeStruct((1,), jnp.int32),
        ),
        in_specs=[SMEM, SMEM, SMEM, HBM, HBM, HBM, HBM, VMEM, VMEM],
        out_specs=(VMEM, SMEM),
        scratch_shapes=[
            pltpu.VMEM((WINDOW, act.shape[1]), jnp.bfloat16),
            pltpu.VMEM((WINDOW, grad.shape[1]), jnp.bfloat16),
            pltpu.VMEM(proj_in.shape, jnp.bfloat16),
            pltpu.VMEM(proj_out.shape, jnp.bfloat16),
            pltpu.SemaphoreType.DMA((10,)),
        ],
        compiler_params=pltpu.CompilerParams(vmem_limit_bytes=16 << 20),
    )(owner, step, lengths, act, grad, proj_in, proj_out, pre_out, pre_in)


def project_kernel(parts, rows_ref, proj_ref, low_ref, rows, proj, sems):
    columns_list = pieces(rows.shape[1], parts)
    copies = []
    for i, columns in enumerate(columns_list):
        pair = (
            pltpu.make_async_copy(proj_ref.at[:, columns], proj.at[:, columns], sems.at[2 * i]),
            pltpu.make_async_copy(rows_ref.at[:, columns], rows.at[:, columns], sems.at[2 * i + 1]),
        )
        for copy in pair:
            copy.start()
        copies.append(pair)
    total = jnp.zeros(low_ref.shape, jnp.float32)
    for columns, pair in zip(columns_list, copies):
        for copy in pair:
            copy.wait()
        total = total + lax.dot_general(
            rows[:, columns], proj[:, columns], NT, preferred_element_type=jnp.float32
        )
    low_ref[...] = total.astype(jnp.bfloat16)


def project(parts, rows, proj):
    tokens, low_rank = rows.shape[0], proj.shape[0]
    return pl.pallas_call(
        functools.partial(project_kernel, parts),
        out_shape=jax.ShapeDtypeStruct((tokens, low_rank), jnp.bfloat16),
        in_specs=[HBM] * 2,
        out_specs=VMEM,
        scratch_shapes=[
            pltpu.VMEM(rows.shape, jnp.bfloat16),
            pltpu.VMEM(proj.shape, jnp.bfloat16),
            pltpu.SemaphoreType.DMA((2 * parts,)),
        ],
        compiler_params=pltpu.CompilerParams(vmem_limit_bytes=16 << 20),
        cost_estimate=pl.CostEstimate(
            flops=2 * low_rank * rows.size, bytes_accessed=2 * (rows.size + proj.size), transcendentals=0
        ),
    )(rows, proj)


def relay_kernel(owner_ref, received_ref, more_ref, out_ref):
    for query in range(owner_ref.shape[0]):
        first = received_ref[line_of(owner_ref[query])]
        value = jnp.where(rank_of(owner_ref, query) == 0, first, more_ref[query])
        out_ref[:, query] = jnp.broadcast_to(value[None], out_ref[:, query].shape)


def relay(peers, owner, received, more):
    return pl.pallas_call(
        relay_kernel,
        out_shape=jax.ShapeDtypeStruct((peers,) + more.shape, more.dtype),
        in_specs=[SMEM, VMEM, VMEM],
        out_specs=VMEM,
    )(owner, received, more)


def score_kernel(owner_ref, lengths_ref, act_ref, grad_ref, received_ref, out_ref, held, sems):
    count = owner_ref.shape[0]
    tokens, low_rank = act_ref.shape
    steps = lengths_ref.shape[1]
    copies = [
        pltpu.make_async_copy(
            received_ref.at[plane_of(owner_ref[query]), query], held.at[query], sems.at[query]
        )
        for query in range(count)
    ]
    for copy in copies:
        copy.start()
    token_of = lax.broadcasted_iota(jnp.int32, (steps, tokens), 1)
    one = lax.broadcasted_iota(jnp.int32, (steps, steps), 0)
    other = lax.broadcasted_iota(jnp.int32, (steps, steps), 1)
    spread = jnp.broadcast_to(lengths_ref[...], (steps, steps))
    begins = jnp.sum(jnp.where(other < one, spread, 0), axis=1, keepdims=True)
    ends = jnp.sum(jnp.where(other <= one, spread, 0), axis=1, keepdims=True)
    member = ((token_of >= begins) & (token_of < ends)).astype(jnp.bfloat16)
    act_low = act_ref[...].astype(jnp.float32)
    act_wide = jnp.concatenate([act_low] * count, axis=1)
    for copy in copies:
        copy.wait()
    weighted = jnp.concatenate(
        [
            jnp.concatenate([held[query][:, :low_rank] for query in range(count)], axis=1),
            jnp.concatenate([held[query][:, low_rank:] for query in range(count)], axis=1),
        ],
        axis=0,
    )
    turned = jnp.dot(grad_ref[...], weighted, preferred_element_type=jnp.float32)
    value = turned * act_wide
    high = value.astype(jnp.bfloat16)
    low = (value - high.astype(jnp.float32)).astype(jnp.bfloat16)
    summed = jnp.dot(member, high, preferred_element_type=jnp.float32) + jnp.dot(
        member, low, preferred_element_type=jnp.float32
    )
    column = lax.broadcasted_iota(jnp.int32, (steps, count * steps), 1)
    row = lax.broadcasted_iota(jnp.int32, (steps, count * steps), 0)
    table = jnp.zeros((steps, count * steps), jnp.float32)
    for query in range(count):
        part = jnp.sum(summed[:, query * low_rank : (query + 1) * low_rank], axis=1, keepdims=True)
        table = jnp.where(column == row + query * steps, part, table)
    out_ref[...] = jnp.broadcast_to(jnp.sum(table, axis=0, keepdims=True), out_ref.shape)


def score(peers, owner, lengths, act_low, grad_low, received):
    count, steps = owner.shape[0], lengths.shape[1]
    return pl.pallas_call(
        score_kernel,
        out_shape=jax.ShapeDtypeStruct((peers, count * steps), jnp.float32),
        in_specs=[SMEM, VMEM, VMEM, VMEM, HBM],
        out_specs=VMEM,
        scratch_shapes=[
            pltpu.VMEM(received.shape[1:], received.dtype),
            pltpu.SemaphoreType.DMA((count,)),
        ],
        compiler_params=pltpu.CompilerParams(vmem_limit_bytes=16 << 20),
    )(owner, lengths, act_low, grad_low, received)


def pick_kernel(layers, scale, retrieval_ref, table_ref, out_ref):
    count, per_scorer = retrieval_ref.shape
    rows, width = table_ref.shape
    steps = width // count
    shift = steps.bit_length() - 1
    ids = retrieval_ref[...]
    wanted = jnp.concatenate([ids[query : query + 1] for query in range(count)], axis=1)
    total = wanted.shape[1]
    source = lax.shift_right_logical(wanted, shift)
    first = lax.broadcasted_iota(jnp.int32, (1, total), 1) // per_scorer * steps
    entry = lax.bitwise_and(wanted, steps - 1) + first
    table_row = lax.broadcasted_iota(jnp.int32, (rows, total), 0) // layers
    chosen = jnp.where(table_row == source, 1.0, 0.0).astype(jnp.bfloat16)
    rest = table_ref[...]
    values = jnp.zeros((width, total), jnp.float32)
    for _ in range(3):
        piece = rest.astype(jnp.bfloat16)
        values = values + lax.dot_general(piece, chosen, TN, preferred_element_type=jnp.float32)
        rest = rest - piece.astype(jnp.float32)
    entry_row = lax.broadcasted_iota(jnp.int32, (width, total), 0)
    found = scale * jnp.sum(jnp.where(entry_row == entry, values, 0.0), axis=0, keepdims=True)
    for query in range(count):
        out_ref[query : query + 1] = found[:, query * per_scorer : (query + 1) * per_scorer]


def pick(layers, scale, retrieval, table):
    return pl.pallas_call(
        functools.partial(pick_kernel, layers, scale),
        out_shape=jax.ShapeDtypeStruct(retrieval.shape, jnp.float32),
        in_specs=[VMEM, VMEM],
        out_specs=VMEM,
    )(retrieval, table)


def local(
    activations,
    out_grads,
    proj_in,
    proj_out,
    precond_out,
    precond_in,
    step_lengths,
    flagged_owner,
    flagged_step,
    retrieval,
):
    low_rank = precond_in.shape[1]
    count = flagged_owner.shape[0]
    layers = lax.axis_size("layer")
    peers = lax.axis_size(DP + ("layer",))
    act, grad = activations[0], out_grads[0]
    into, outof = proj_in[0].T, proj_out[0].T

    def swap(value, axes):
        return lax.all_to_all(value, axes, split_axis=0, concat_axis=0, tiled=True)

    def own_slot(slot):
        return flagged(
            slot, SIZES[1], flagged_owner, flagged_step, step_lengths,
            act, grad, into, outof, precond_out[0], precond_in[0],
        )

    def further_rounds():
        earlier = jnp.arange(count)[None, :] < jnp.arange(count)[:, None]
        same = flagged_owner[:, None] == flagged_owner[None, :]
        ranks = jnp.sum((earlier & same).astype(jnp.int32), axis=1)
        rounds = jnp.stack(
            [swap(own_slot(slot)[0], "z")[line_of(flagged_owner)] for slot in range(1, count)]
        )
        return rounds[jnp.maximum(ranks - 1, 0), jnp.arange(count)]

    def no_further():
        return jnp.zeros((count, low_rank // 2, 2 * low_rank), jnp.bfloat16)

    own, again = own_slot(0)
    in_line = swap(own, "z")
    more = lax.cond(again[0] > 0, further_rounds, no_further)
    act_low = project(6, act, into)
    plane = relay(SIZES[0] * SIZES[2], flagged_owner, in_line, more)
    in_plane = swap(plane, PLANE)
    grad_low = project(4, grad, outof)
    table = score(peers, flagged_owner, step_lengths, act_low, grad_low, in_plane)
    tables = swap(table, DP + ("layer",))
    return pick(layers, 1.0 / (low_rank * STEP_MAX), retrieval, tables)


def solution(mesh):
    parts = Mesh(mesh.devices.reshape(SIZES + (mesh.shape["layer"],)), DP + ("layer",))
    return jax.shard_map(
        local,
        mesh=parts,
        in_specs=(
            P("layer", DP, None),
            P("layer", DP, None),
            P("layer", None, None),
            P("layer", None, None),
            P("layer", None, None),
            P("layer", None, None),
            P(DP, None),
            P(),
            P(),
            P(None, DP),
        ),
        out_specs=P(None, DP),
        check_vma=False,
    )
```

```python
import functools

import jax
import jax.numpy as jnp
from jax import lax
from jax.experimental import pallas as pl
from jax.experimental.pallas import tpu as pltpu
from jax.sharding import Mesh, PartitionSpec as P

WINDOW = 80
ALIGN = 16
STEP_MAX = 64
SIZES = (4, 8, 4)
DP = ("y", "z", "x")
PLANE = ("y", "x")
NT = (((1,), (1,)), ((), ()))
TN = (((0,), (0,)), ((), ()))
HIGHEST = lax.Precision.HIGHEST
SMEM = pl.BlockSpec(memory_space=pltpu.SMEM)
VMEM = pl.BlockSpec(memory_space=pltpu.VMEM)
HBM = pl.BlockSpec(memory_space=pl.ANY)


def rank_of(owner_ref, query):
    rank = jnp.int32(0)
    for other in range(query):
        rank = rank + jnp.where(owner_ref[other] == owner_ref[query], 1, 0).astype(jnp.int32)
    return rank


def line_of(owner):
    return lax.rem(lax.div(owner, SIZES[2]), SIZES[1])


def plane_of(owner):
    return lax.div(owner, SIZES[1] * SIZES[2]) * SIZES[2] + lax.rem(owner, SIZES[2])


def pieces(total, count):
    width = total // count
    return [pl.ds(i * width, width) for i in range(count)]


def flagged_kernel(
    slot,
    owner_ref,
    step_ref,
    lengths_ref,
    act_ref,
    grad_ref,
    proj_in_ref,
    proj_out_ref,
    precond_out_ref,
    precond_in_ref,
    out_ref,
    act_rows,
    grad_rows,
    proj_in,
    proj_out,
    sems,
):
    me = lax.axis_index(DP)
    low_rank = proj_in.shape[0]
    half = low_rank // 2
    tokens = act_ref.shape[0]
    mine = jnp.int32(-1)
    for query in range(owner_ref.shape[0]):
        rank = rank_of(owner_ref, query)
        mine = jnp.where((owner_ref[query] == me) & (rank == slot), step_ref[query], mine)

    @pl.when(mine < 0)
    def _():
        out_ref[...] = jnp.zeros_like(out_ref)

    @pl.when(mine >= 0)
    def _():
        begin = jnp.int32(0)
        for step in range(lengths_ref.shape[1]):
            begin = begin + jnp.where(step < mine, lengths_ref[0, step], 0)
        end = begin + lengths_ref[0, mine]
        first = jnp.minimum(begin // ALIGN, (tokens - WINDOW) // ALIGN) * ALIGN
        rows = pl.ds(pl.multiple_of(first, ALIGN), WINDOW)
        act_cols = pieces(act_ref.shape[1], 6)
        grad_cols = pieces(grad_ref.shape[1], 4)
        copies = []
        for columns, source, held, weights, held_weights in (
            [(c, act_ref, act_rows, proj_in_ref, proj_in) for c in act_cols]
            + [(c, grad_ref, grad_rows, proj_out_ref, proj_out) for c in grad_cols]
        ):
            pair = (
                pltpu.make_async_copy(
                    weights.at[:, columns], held_weights.at[:, columns], sems.at[2 * len(copies)]
                ),
                pltpu.make_async_copy(
                    source.at[rows, columns], held.at[:, columns], sems.at[2 * len(copies) + 1]
                ),
            )
            for copy in pair:
                copy.start()
            copies.append(pair)
        lows = []
        done = 0
        for columns_list, held, held_weights in (
            (act_cols, act_rows, proj_in),
            (grad_cols, grad_rows, proj_out),
        ):
            total = jnp.zeros((WINDOW, low_rank), jnp.float32)
            for columns in columns_list:
                for copy in copies[done]:
                    copy.wait()
                done += 1
                total = total + lax.dot_general(
                    held[:, columns],
                    held_weights[:, columns],
                    NT,
                    preferred_element_type=jnp.float32,
                )
            lows.append(total)
        position = first + lax.broadcasted_iota(jnp.int32, (WINDOW, low_rank), 0)
        inside = (position >= begin) & (position < end)
        act_low = lows[0].astype(jnp.bfloat16)
        grad_low = jnp.where(inside, lows[1], 0.0).astype(jnp.bfloat16)
        step_grad = lax.dot_general(grad_low, act_low, TN, preferred_element_type=jnp.float32)
        step_grad = step_grad.astype(jnp.bfloat16).astype(jnp.float32)
        left = jnp.dot(
            precond_out_ref[...], step_grad, precision=HIGHEST, preferred_element_type=jnp.float32
        )
        both = jnp.dot(
            left, precond_in_ref[...], precision=HIGHEST, preferred_element_type=jnp.float32
        )
        packed = jnp.concatenate([both[:half], both[half:]], axis=1).astype(jnp.bfloat16)
        out_ref[...] = jnp.broadcast_to(packed[None], out_ref.shape)


def flagged(slot, peers, owner, step, lengths, act, grad, proj_in, proj_out, pre_out, pre_in):
    low_rank = proj_in.shape[0]
    return pl.pallas_call(
        functools.partial(flagged_kernel, slot),
        out_shape=jax.ShapeDtypeStruct((peers, low_rank // 2, 2 * low_rank), jnp.bfloat16),
        in_specs=[SMEM, SMEM, SMEM, HBM, HBM, HBM, HBM, VMEM, VMEM],
        out_specs=VMEM,
        scratch_shapes=[
            pltpu.VMEM((WINDOW, act.shape[1]), jnp.bfloat16),
            pltpu.VMEM((WINDOW, grad.shape[1]), jnp.bfloat16),
            pltpu.VMEM(proj_in.shape, jnp.bfloat16),
            pltpu.VMEM(proj_out.shape, jnp.bfloat16),
            pltpu.SemaphoreType.DMA((20,)),
        ],
        compiler_params=pltpu.CompilerParams(vmem_limit_bytes=16 << 20),
    )(owner, step, lengths, act, grad, proj_in, proj_out, pre_out, pre_in)


def project_kernel(rows_ref, proj_ref, low_ref):
    low_ref[...] = lax.dot_general(
        rows_ref[...], proj_ref[...], NT, preferred_element_type=jnp.float32
    ).astype(jnp.bfloat16)


def project(rows, proj):
    tokens, low_rank = rows.shape[0], proj.shape[0]
    return pl.pallas_call(
        project_kernel,
        out_shape=jax.ShapeDtypeStruct((tokens, low_rank), jnp.bfloat16),
        in_specs=[VMEM] * 2,
        out_specs=VMEM,
        compiler_params=pltpu.CompilerParams(vmem_limit_bytes=8 << 20),
        cost_estimate=pl.CostEstimate(
            flops=2 * low_rank * rows.size, bytes_accessed=2 * rows.size, transcendentals=0
        ),
    )(rows, proj)


def relay_one_kernel(owner_ref, received_ref, out_ref):
    here = plane_of(lax.axis_index(DP))
    slot = jnp.int32(0)
    for query in range(owner_ref.shape[0]):
        slot = jnp.where(plane_of(owner_ref[query]) == here, line_of(owner_ref[query]), slot)
    out_ref[...] = jnp.broadcast_to(received_ref[slot][None], out_ref.shape)


def relay_one(peers, owner, received):
    return pl.pallas_call(
        relay_one_kernel,
        out_shape=jax.ShapeDtypeStruct((peers,) + received.shape[1:], received.dtype),
        in_specs=[SMEM, VMEM],
        out_specs=VMEM,
        compiler_params=pltpu.CompilerParams(vmem_limit_bytes=4 << 20),
    )(owner, received)


def relay_kernel(owner_ref, received_ref, more_ref, out_ref):
    for query in range(owner_ref.shape[0]):
        first = received_ref[line_of(owner_ref[query])]
        value = jnp.where(rank_of(owner_ref, query) == 0, first, more_ref[query])
        out_ref[:, query] = jnp.broadcast_to(value[None], out_ref[:, query].shape)


def relay(peers, owner, received, more):
    return pl.pallas_call(
        relay_kernel,
        out_shape=jax.ShapeDtypeStruct((peers,) + more.shape, more.dtype),
        in_specs=[SMEM, VMEM, VMEM],
        out_specs=VMEM,
        compiler_params=pltpu.CompilerParams(vmem_limit_bytes=4 << 20),
    )(owner, received, more)


def score_kernel(owner_ref, lengths_ref, act_ref, grad_ref, received_ref, out_ref, held, sems):
    count = owner_ref.shape[0]
    tokens, low_rank = act_ref.shape
    steps = lengths_ref.shape[1]
    copies = [
        pltpu.make_async_copy(
            (
                received_ref.at[plane_of(owner_ref[query]), query]
                if len(received_ref.shape) == 4
                else received_ref.at[plane_of(owner_ref[query])]
            ),
            held.at[query],
            sems.at[query],
        )
        for query in range(count)
    ]
    for copy in copies:
        copy.start()
    token_of = lax.broadcasted_iota(jnp.int32, (steps, tokens), 1)
    one = lax.broadcasted_iota(jnp.int32, (steps, steps), 0)
    other = lax.broadcasted_iota(jnp.int32, (steps, steps), 1)
    spread = jnp.broadcast_to(lengths_ref[...], (steps, steps))
    begins = jnp.sum(jnp.where(other < one, spread, 0), axis=1, keepdims=True)
    ends = jnp.sum(jnp.where(other <= one, spread, 0), axis=1, keepdims=True)
    member = ((token_of >= begins) & (token_of < ends)).astype(jnp.bfloat16)
    act_low = act_ref[...].astype(jnp.float32)
    act_wide = jnp.concatenate([act_low] * count, axis=1)
    for copy in copies:
        copy.wait()
    weighted = jnp.concatenate(
        [
            jnp.concatenate([held[query][:, :low_rank] for query in range(count)], axis=1),
            jnp.concatenate([held[query][:, low_rank:] for query in range(count)], axis=1),
        ],
        axis=0,
    )
    turned = jnp.dot(grad_ref[...], weighted, preferred_element_type=jnp.float32)
    value = turned * act_wide
    high = value.astype(jnp.bfloat16)
    low = (value - high.astype(jnp.float32)).astype(jnp.bfloat16)
    summed = jnp.dot(member, high, preferred_element_type=jnp.float32) + jnp.dot(
        member, low, preferred_element_type=jnp.float32
    )
    column = lax.broadcasted_iota(jnp.int32, (steps, count * steps), 1)
    row = lax.broadcasted_iota(jnp.int32, (steps, count * steps), 0)
    table = jnp.zeros((steps, count * steps), jnp.float32)
    for query in range(count):
        part = jnp.sum(summed[:, query * low_rank : (query + 1) * low_rank], axis=1, keepdims=True)
        table = jnp.where(column == row + query * steps, part, table)
    out_ref[...] = jnp.broadcast_to(jnp.sum(table, axis=0, keepdims=True), out_ref.shape)


def score(peers, owner, lengths, act_low, grad_low, received):
    count, steps = owner.shape[0], lengths.shape[1]
    return pl.pallas_call(
        score_kernel,
        out_shape=jax.ShapeDtypeStruct((peers, count * steps), jnp.float32),
        in_specs=[SMEM, VMEM, VMEM, VMEM, HBM],
        out_specs=VMEM,
        scratch_shapes=[
            pltpu.VMEM((count,) + received.shape[-2:], received.dtype),
            pltpu.SemaphoreType.DMA((count,)),
        ],
        compiler_params=pltpu.CompilerParams(vmem_limit_bytes=16 << 20),
    )(owner, lengths, act_low, grad_low, received)


def pick_kernel(layers, scale, retrieval_ref, table_ref, out_ref):
    count, per_scorer = retrieval_ref.shape
    rows, width = table_ref.shape
    steps = width // count
    shift = steps.bit_length() - 1
    ids = retrieval_ref[...]
    wanted = jnp.concatenate([ids[query : query + 1] for query in range(count)], axis=1)
    total = wanted.shape[1]
    source = lax.shift_right_logical(wanted, shift)
    first = lax.broadcasted_iota(jnp.int32, (1, total), 1) // per_scorer * steps
    entry = lax.bitwise_and(wanted, steps - 1) + first
    table_row = lax.broadcasted_iota(jnp.int32, (rows, total), 0) // layers
    chosen = jnp.where(table_row == source, 1.0, 0.0).astype(jnp.bfloat16)
    rest = table_ref[...]
    values = jnp.zeros((width, total), jnp.float32)
    for _ in range(3):
        piece = rest.astype(jnp.bfloat16)
        values = values + lax.dot_general(piece, chosen, TN, preferred_element_type=jnp.float32)
        rest = rest - piece.astype(jnp.float32)
    entry_row = lax.broadcasted_iota(jnp.int32, (width, total), 0)
    found = scale * jnp.sum(jnp.where(entry_row == entry, values, 0.0), axis=0, keepdims=True)
    for query in range(count):
        out_ref[query : query + 1] = found[:, query * per_scorer : (query + 1) * per_scorer]


def pick(layers, scale, retrieval, table):
    return pl.pallas_call(
        functools.partial(pick_kernel, layers, scale),
        out_shape=jax.ShapeDtypeStruct(retrieval.shape, jnp.float32),
        in_specs=[VMEM, VMEM],
        out_specs=VMEM,
        compiler_params=pltpu.CompilerParams(vmem_limit_bytes=4 << 20),
    )(retrieval, table)


def local(
    activations,
    out_grads,
    proj_in,
    proj_out,
    precond_out,
    precond_in,
    step_lengths,
    flagged_owner,
    flagged_step,
    retrieval,
):
    low_rank = precond_in.shape[1]
    count = flagged_owner.shape[0]
    layers = lax.axis_size("layer")
    peers = lax.axis_size(DP + ("layer",))
    act, grad = activations[0], out_grads[0]
    into, outof = proj_in[0].T, proj_out[0].T

    def swap(value, axes):
        return lax.all_to_all(value, axes, split_axis=0, concat_axis=0, tiled=True)

    def own_slot(slot):
        return flagged(
            slot, SIZES[1], flagged_owner, flagged_step, step_lengths,
            act, grad, into, outof, precond_out[0], precond_in[0],
        )

    def earlier_twins(owners):
        earlier = jnp.arange(count)[None, :] < jnp.arange(count)[:, None]
        same = owners[:, None] == owners[None, :]
        return (earlier & same).astype(jnp.int32)

    def further_rounds():
        rounds = jnp.stack(
            [swap(own_slot(slot), "z")[line_of(flagged_owner)] for slot in range(1, count)]
        )
        return rounds[jnp.maximum(jnp.sum(earlier_twins(flagged_owner), axis=1) - 1, 0), jnp.arange(count)]

    def no_further():
        return jnp.zeros((count, low_rank // 2, 2 * low_rank), jnp.bfloat16)

    def scored(plane, cols):
        in_plane = swap(plane, PLANE)
        grad_low = project(cols, outof)
        in_plane, grad_low = lax.optimization_barrier((in_plane, grad_low))
        return score(peers, flagged_owner, step_lengths, act_low, grad_low, in_plane)

    def one_a_line(in_line, cols):
        return scored(relay_one(width, flagged_owner, in_line), cols)

    def several_a_line(in_line, cols):
        more = lax.cond(
            jnp.max(earlier_twins(flagged_owner)) > 0, further_rounds, no_further
        )
        return scored(relay(width, flagged_owner, in_line, more), cols)

    width = SIZES[0] * SIZES[2]
    own = own_slot(0)
    in_line = swap(own, "z")
    act_low = project(act, into)
    owners, act_low = lax.optimization_barrier((flagged_owner, act_low))
    several = jnp.max(earlier_twins(plane_of(owners))) > 0
    in_line, several, act_low, cols = lax.optimization_barrier((in_line, several, act_low, grad))
    table = lax.cond(several, several_a_line, one_a_line, in_line, cols)
    tables = swap(table, DP + ("layer",))
    return pick(layers, 1.0 / (low_rank * STEP_MAX), retrieval, tables)


def solution(mesh):
    parts = Mesh(mesh.devices.reshape(SIZES + (mesh.shape["layer"],)), DP + ("layer",))
    return jax.shard_map(
        local,
        mesh=parts,
        in_specs=(
            P("layer", DP, None),
            P("layer", DP, None),
            P("layer", None, None),
            P("layer", None, None),
            P("layer", None, None),
            P("layer", None, None),
            P(DP, None),
            P(),
            P(),
            P(None, DP),
        ),
        out_specs=P(None, DP),
        check_vma=False,
    )
```

```python
import functools

import jax
import jax.numpy as jnp
from jax import lax
from jax.experimental import pallas as pl
from jax.experimental.pallas import tpu as pltpu
from jax.sharding import Mesh, PartitionSpec as P

WINDOW = 80
ALIGN = 16
STEP_MAX = 64
SIZES = (4, 8, 4)
DP = ("y", "z", "x")
PLANE = ("y", "x")
NT = (((1,), (1,)), ((), ()))
TN = (((0,), (0,)), ((), ()))
HIGHEST = lax.Precision.HIGHEST
SMEM = pl.BlockSpec(memory_space=pltpu.SMEM)
VMEM = pl.BlockSpec(memory_space=pltpu.VMEM)
HBM = pl.BlockSpec(memory_space=pl.ANY)


def rank_of(owner_ref, query):
    rank = jnp.int32(0)
    for other in range(query):
        rank = rank + jnp.where(owner_ref[other] == owner_ref[query], 1, 0).astype(jnp.int32)
    return rank


def line_of(owner):
    return lax.rem(lax.div(owner, SIZES[2]), SIZES[1])


def plane_of(owner):
    return lax.div(owner, SIZES[1] * SIZES[2]) * SIZES[2] + lax.rem(owner, SIZES[2])


def pieces(total, count):
    width = total // count
    return [pl.ds(i * width, width) for i in range(count)]


def flagged_kernel(
    slot,
    owner_ref,
    step_ref,
    lengths_ref,
    act_ref,
    grad_ref,
    proj_in_ref,
    proj_out_ref,
    precond_out_ref,
    precond_in_ref,
    out_ref,
    several_ref,
    owners,
    steps,
    lengths,
    act_rows,
    grad_rows,
    proj_in,
    proj_out,
    precond_out,
    precond_in,
    sems,
    row_sems,
):
    scalars = [
        pltpu.make_async_copy(source, held, sems.at[i])
        for i, (source, held) in enumerate(
            ((owner_ref, owners), (step_ref, steps), (lengths_ref, lengths))
        )
    ]
    weights = [
        pltpu.make_async_copy(source, held, sems.at[3 + i])
        for i, (source, held) in enumerate(
            (
                (proj_in_ref, proj_in),
                (proj_out_ref, proj_out),
                (precond_out_ref, precond_out),
                (precond_in_ref, precond_in),
            )
        )
    ]
    for copy in scalars + weights:
        copy.start()
    me = lax.axis_index(DP)
    low_rank = proj_in.shape[0]
    half = low_rank // 2
    tokens = act_ref.shape[0]
    for copy in scalars:
        copy.wait()
    mine = jnp.int32(-1)
    several = jnp.int32(0)
    for query in range(owners.shape[0]):
        rank = rank_of(owners, query)
        mine = jnp.where((owners[query] == me) & (rank == slot), steps[query], mine)
        for other in range(query):
            shared = plane_of(owners[query]) == plane_of(owners[other])
            several = jnp.where(shared, 1, several)
    several_ref[0] = several

    @pl.when(mine < 0)
    def _():
        out_ref[...] = jnp.zeros_like(out_ref)
        for copy in weights:
            copy.wait()

    @pl.when(mine >= 0)
    def _():
        begin = jnp.int32(0)
        for step in range(lengths.shape[1]):
            begin = begin + jnp.where(step < mine, lengths[0, step], 0)
        end = begin + lengths[0, mine]
        first = jnp.minimum(lax.div(begin, ALIGN), (tokens - WINDOW) // ALIGN) * ALIGN

        def tile(index, which):
            source, held = ((act_ref, act_rows), (grad_ref, grad_rows))[which]
            start = pl.multiple_of(first + index * ALIGN, ALIGN)
            return pltpu.make_async_copy(
                source.at[pl.ds(start, ALIGN)],
                held.at[pl.ds(index * ALIGN, ALIGN)],
                row_sems.at[which, index],
            )

        def each_tile(which, act):
            for index in range(WINDOW // ALIGN):

                @pl.when(first + index * ALIGN < end)
                def _():
                    act(tile(index, which))

        for which in range(2):
            each_tile(which, lambda copy: copy.start())
        for copy in weights[2:]:
            copy.wait()

        def finish(size):
            position = first + lax.broadcasted_iota(jnp.int32, (size, low_rank), 0)
            inside = (position >= begin) & (position < end)
            lows = []
            for which, (held, held_weights) in enumerate(
                ((act_rows, proj_in), (grad_rows, proj_out))
            ):
                weights[which].wait()
                each_tile(which, lambda copy: copy.wait())
                low = lax.dot_general(
                    held[:size], held_weights[...], NT, preferred_element_type=jnp.float32
                )
                lows.append(jnp.where(inside, low, 0.0).astype(jnp.bfloat16))
            step_grad = lax.dot_general(lows[1], lows[0], TN, preferred_element_type=jnp.float32)
            step_grad = step_grad.astype(jnp.bfloat16).astype(jnp.float32)
            left = jnp.dot(
                precond_out[...], step_grad, precision=HIGHEST, preferred_element_type=jnp.float32
            )
            both = jnp.dot(
                left, precond_in[...], precision=HIGHEST, preferred_element_type=jnp.float32
            ).T
            packed = jnp.concatenate([both[:half], both[half:]], axis=1).astype(jnp.bfloat16)
            out_ref[...] = jnp.broadcast_to(packed[None], out_ref.shape)

        small = end - first <= 2 * ALIGN

        @pl.when(small)
        def _():
            finish(2 * ALIGN)

        @pl.when(jnp.logical_not(small))
        def _():
            finish(WINDOW)


def flagged(slot, peers, owner, step, lengths, act, grad, proj_in, proj_out, pre_out, pre_in):
    low_rank = proj_in.shape[0]
    return pl.pallas_call(
        functools.partial(flagged_kernel, slot),
        out_shape=(
            jax.ShapeDtypeStruct((peers, low_rank // 2, 2 * low_rank), jnp.bfloat16),
            jax.ShapeDtypeStruct((1,), jnp.int32),
        ),
        in_specs=[HBM] * 9,
        out_specs=(VMEM, SMEM),
        scratch_shapes=[
            pltpu.SMEM(owner.shape, jnp.int32),
            pltpu.SMEM(step.shape, jnp.int32),
            pltpu.SMEM(lengths.shape, jnp.int32),
            pltpu.VMEM((WINDOW, act.shape[1]), jnp.bfloat16),
            pltpu.VMEM((WINDOW, grad.shape[1]), jnp.bfloat16),
            pltpu.VMEM(proj_in.shape, jnp.bfloat16),
            pltpu.VMEM(proj_out.shape, jnp.bfloat16),
            pltpu.VMEM(pre_out.shape, jnp.float32),
            pltpu.VMEM(pre_in.shape, jnp.float32),
            pltpu.SemaphoreType.DMA((7,)),
            pltpu.SemaphoreType.DMA((2, WINDOW // ALIGN)),
        ],
        compiler_params=pltpu.CompilerParams(vmem_limit_bytes=8 << 20),
    )(owner, step, lengths, act, grad, proj_in, proj_out, pre_out, pre_in)


def turned_dot(rows_ref, proj_ref):
    low = lax.dot_general(rows_ref[...], proj_ref[...], NT, preferred_element_type=jnp.float32)
    return low.astype(jnp.bfloat16).astype(jnp.float32).T.astype(jnp.bfloat16)


def project_act_kernel(rows_ref, proj_ref, low_ref):
    low_ref[...] = turned_dot(rows_ref, proj_ref)


def project_grad_kernel(rows_ref, proj_ref, lengths_ref, low_ref, member_ref):
    steps, tokens = member_ref.shape
    token_of = lax.broadcasted_iota(jnp.int32, (steps, tokens), 1)
    one = lax.broadcasted_iota(jnp.int32, (steps, steps), 0)
    other = lax.broadcasted_iota(jnp.int32, (steps, steps), 1)
    spread = jnp.broadcast_to(lengths_ref[...], (steps, steps))
    begins = jnp.sum(jnp.where(other < one, spread, 0), axis=1, keepdims=True)
    ends = jnp.sum(jnp.where(other <= one, spread, 0), axis=1, keepdims=True)
    member_ref[...] = ((token_of >= begins) & (token_of < ends)).astype(jnp.bfloat16)
    low_ref[...] = turned_dot(rows_ref, proj_ref)


def project(rows, proj, lengths=None):
    tokens, low_rank = rows.shape[0], proj.shape[0]
    low = jax.ShapeDtypeStruct((low_rank, tokens), jnp.bfloat16)
    options = dict(
        compiler_params=pltpu.CompilerParams(vmem_limit_bytes=8 << 20),
        cost_estimate=pl.CostEstimate(
            flops=2 * low_rank * rows.size, bytes_accessed=2 * rows.size, transcendentals=0
        ),
    )
    if lengths is None:
        return pl.pallas_call(
            project_act_kernel, out_shape=low, in_specs=[VMEM] * 2, out_specs=VMEM, **options
        )(rows, proj)
    member = jax.ShapeDtypeStruct((lengths.shape[1], tokens), jnp.bfloat16)
    return pl.pallas_call(
        project_grad_kernel,
        out_shape=(low, member),
        in_specs=[VMEM] * 3,
        out_specs=(VMEM, VMEM),
        **options,
    )(rows, proj, lengths)


def relay_one_kernel(received_ref, out_ref):
    only = jnp.sum(received_ref[...].astype(jnp.float32), axis=0).astype(jnp.bfloat16)
    out_ref[...] = jnp.broadcast_to(only[None], out_ref.shape)


def relay_one(peers, received):
    return pl.pallas_call(
        relay_one_kernel,
        out_shape=jax.ShapeDtypeStruct((peers,) + received.shape[1:], received.dtype),
        in_specs=[VMEM],
        out_specs=VMEM,
        compiler_params=pltpu.CompilerParams(vmem_limit_bytes=4 << 20),
    )(received)


def relay_kernel(owner_ref, received_ref, more_ref, out_ref):
    for query in range(owner_ref.shape[0]):
        first = received_ref[line_of(owner_ref[query])]
        value = jnp.where(rank_of(owner_ref, query) == 0, first, more_ref[query])
        out_ref[:, query] = jnp.broadcast_to(value[None], out_ref[:, query].shape)


def relay(peers, owner, received, more):
    return pl.pallas_call(
        relay_kernel,
        out_shape=jax.ShapeDtypeStruct((peers,) + more.shape, more.dtype),
        in_specs=[SMEM, VMEM, VMEM],
        out_specs=VMEM,
        compiler_params=pltpu.CompilerParams(vmem_limit_bytes=4 << 20),
    )(owner, received, more)


def score_kernel(owner_ref, act_ref, grad_ref, member_ref, received_ref, out_ref):
    count = owner_ref.shape[0]
    low_rank, tokens = act_ref.shape
    steps = member_ref.shape[0]
    held = []
    for query in range(count):
        place = plane_of(owner_ref[query])
        packed = (
            received_ref[place, query] if len(received_ref.shape) == 4 else received_ref[place]
        )
        held += [packed[:, :low_rank], packed[:, low_rank:]]
    weighted = jnp.concatenate(held, axis=0)
    turned = jnp.dot(weighted, grad_ref[...], preferred_element_type=jnp.float32)
    act_low = act_ref[...].astype(jnp.float32)
    value = turned.reshape(count, low_rank, tokens) * act_low[None]
    value = value.reshape(count * low_rank, tokens)
    high = value.astype(jnp.bfloat16)
    low = (value - high.astype(jnp.float32)).astype(jnp.bfloat16)
    member = member_ref[...]
    summed = lax.dot_general(
        high, member, NT, preferred_element_type=jnp.float32
    ) + lax.dot_general(low, member, NT, preferred_element_type=jnp.float32)
    table = jnp.sum(summed.reshape(count, low_rank, steps), axis=1)
    row = jnp.concatenate([table[query : query + 1] for query in range(count)], axis=1)
    out_ref[...] = jnp.broadcast_to(row, out_ref.shape)


def score(peers, owner, act_low, grad_low, member, received):
    count, steps = owner.shape[0], member.shape[0]
    return pl.pallas_call(
        score_kernel,
        out_shape=jax.ShapeDtypeStruct((peers, count * steps), jnp.float32),
        in_specs=[SMEM, VMEM, VMEM, VMEM, VMEM],
        out_specs=VMEM,
        compiler_params=pltpu.CompilerParams(vmem_limit_bytes=8 << 20),
    )(owner, act_low, grad_low, member, received)


def pick_kernel(layers, scale, retrieval_ref, table_ref, out_ref):
    count, per_scorer = retrieval_ref.shape
    rows, width = table_ref.shape
    steps = width // count
    shift = steps.bit_length() - 1
    ids = retrieval_ref[...]
    wanted = jnp.concatenate([ids[query : query + 1] for query in range(count)], axis=1)
    total = wanted.shape[1]
    source = lax.shift_right_logical(wanted, shift)
    first = lax.broadcasted_iota(jnp.int32, (1, total), 1) // per_scorer * steps
    entry = lax.bitwise_and(wanted, steps - 1) + first
    table_row = lax.broadcasted_iota(jnp.int32, (rows, total), 0) // layers
    chosen = jnp.where(table_row == source, 1.0, 0.0).astype(jnp.bfloat16)
    rest = table_ref[...]
    values = jnp.zeros((width, total), jnp.float32)
    for _ in range(3):
        piece = rest.astype(jnp.bfloat16)
        values = values + lax.dot_general(piece, chosen, TN, preferred_element_type=jnp.float32)
        rest = rest - piece.astype(jnp.float32)
    entry_row = lax.broadcasted_iota(jnp.int32, (width, total), 0)
    found = scale * jnp.sum(jnp.where(entry_row == entry, values, 0.0), axis=0, keepdims=True)
    for query in range(count):
        out_ref[query : query + 1] = found[:, query * per_scorer : (query + 1) * per_scorer]


def pick(layers, scale, retrieval, table):
    return pl.pallas_call(
        functools.partial(pick_kernel, layers, scale),
        out_shape=jax.ShapeDtypeStruct(retrieval.shape, jnp.float32),
        in_specs=[VMEM, VMEM],
        out_specs=VMEM,
        compiler_params=pltpu.CompilerParams(vmem_limit_bytes=4 << 20),
    )(retrieval, table)


def local(
    activations,
    out_grads,
    proj_in,
    proj_out,
    precond_out,
    precond_in,
    step_lengths,
    flagged_owner,
    flagged_step,
    retrieval,
):
    low_rank = precond_in.shape[1]
    count = flagged_owner.shape[0]
    layers = lax.axis_size("layer")
    peers = lax.axis_size(DP + ("layer",))
    act, grad = activations[0], out_grads[0]
    into, outof = proj_in[0].T, proj_out[0].T

    def swap(value, axes):
        return lax.all_to_all(value, axes, split_axis=0, concat_axis=0, tiled=True)

    def own_slot(slot):
        return flagged(
            slot, SIZES[1], flagged_owner, flagged_step, step_lengths,
            act, grad, into, outof, precond_out[0], precond_in[0],
        )

    def earlier_twins(owners):
        earlier = jnp.arange(count)[None, :] < jnp.arange(count)[:, None]
        same = owners[:, None] == owners[None, :]
        return (earlier & same).astype(jnp.int32)

    def further_rounds():
        rounds = jnp.stack(
            [swap(own_slot(slot)[0], "z")[line_of(flagged_owner)] for slot in range(1, count)]
        )
        return rounds[jnp.maximum(jnp.sum(earlier_twins(flagged_owner), axis=1) - 1, 0), jnp.arange(count)]

    def no_further():
        return jnp.zeros((count, low_rank // 2, 2 * low_rank), jnp.bfloat16)

    def scored(plane, cols):
        in_plane = swap(plane, PLANE)
        grad_low, member = project(cols, outof, step_lengths)
        in_plane, grad_low, member = lax.optimization_barrier((in_plane, grad_low, member))
        return score(peers, flagged_owner, act_low, grad_low, member, in_plane)

    def one_a_line(in_line, cols):
        return scored(relay_one(width, in_line), cols)

    def several_a_line(in_line, cols):
        more = lax.cond(
            jnp.max(earlier_twins(flagged_owner)) > 0, further_rounds, no_further
        )
        return scored(relay(width, flagged_owner, in_line, more), cols)

    width = SIZES[0] * SIZES[2]
    own, several = own_slot(0)
    in_line = swap(own, "z")
    act_low = project(act, into)
    several, act_low = lax.optimization_barrier((several, act_low))
    several = several[0] > 0
    in_line, several, act_low, cols = lax.optimization_barrier((in_line, several, act_low, grad))
    table = lax.cond(several, several_a_line, one_a_line, in_line, cols)
    tables = swap(table, DP + ("layer",))
    return pick(layers, 1.0 / (low_rank * STEP_MAX), retrieval, tables)


def solution(mesh):
    parts = Mesh(mesh.devices.reshape(SIZES + (mesh.shape["layer"],)), DP + ("layer",))
    return jax.shard_map(
        local,
        mesh=parts,
        in_specs=(
            P("layer", DP, None),
            P("layer", DP, None),
            P("layer", None, None),
            P("layer", None, None),
            P("layer", None, None),
            P("layer", None, None),
            P(DP, None),
            P(),
            P(),
            P(None, DP),
        ),
        out_specs=P(None, DP),
        check_vma=False,
    )
```

```python
import functools

import jax
import jax.numpy as jnp
from jax import lax
from jax.experimental import pallas as pl
from jax.experimental.pallas import tpu as pltpu
from jax.sharding import Mesh, PartitionSpec as P

WINDOW = 80
SMALL = 32
TWINS = 4
ALIGN = 16
BLOCKS = 2
STEP_MAX = 64
SIZES = (4, 8, 4)
DP = ("y", "z", "x")
PLANE = ("y", "x")
NT = (((1,), (1,)), ((), ()))
TN = (((0,), (0,)), ((), ()))
HIGHEST = lax.Precision.HIGHEST
SMEM = pl.BlockSpec(memory_space=pltpu.SMEM)
VMEM = pl.BlockSpec(memory_space=pltpu.VMEM)
HBM = pl.BlockSpec(memory_space=pl.ANY)


def rank_of(owner_ref, query):
    rank = jnp.int32(0)
    for other in range(query):
        rank = rank + jnp.where(owner_ref[other] == owner_ref[query], 1, 0).astype(jnp.int32)
    return rank


def bits(size):
    return size.bit_length() - 1


def line_of(owner):
    return lax.bitwise_and(lax.shift_right_logical(owner, bits(SIZES[2])), SIZES[1] - 1)


def plane_of(owner):
    row = lax.shift_right_logical(owner, bits(SIZES[1] * SIZES[2]))
    return row * SIZES[2] + lax.bitwise_and(owner, SIZES[2] - 1)


def line_rank(owner_ref, query):
    rank = jnp.int32(0)
    for other in range(query):
        shared = plane_of(owner_ref[other]) == plane_of(owner_ref[query])
        rank = rank + jnp.where(shared, 1, 0).astype(jnp.int32)
    return rank


def flagged_kernel(
    slot,
    owner_ref,
    step_ref,
    lengths_ref,
    act_ref,
    grad_ref,
    proj_in_ref,
    proj_out_ref,
    precond_out_ref,
    precond_in_ref,
    out_ref,
    sharing_ref,
    owners,
    steps,
    lengths,
    act_rows,
    grad_rows,
    proj_in,
    proj_out,
    precond_out,
    precond_in,
    sems,
    row_sems,
):
    scalars = [
        pltpu.make_async_copy(source, held, sems.at[i])
        for i, (source, held) in enumerate(
            ((owner_ref, owners), (step_ref, steps), (lengths_ref, lengths))
        )
    ]
    weights = [
        pltpu.make_async_copy(source, held, sems.at[3 + i])
        for i, (source, held) in enumerate(
            (
                (proj_in_ref, proj_in),
                (proj_out_ref, proj_out),
                (precond_out_ref, precond_out),
                (precond_in_ref, precond_in),
            )
        )
    ]
    for copy in scalars + weights:
        copy.start()
    me = lax.axis_index(DP)
    low_rank = proj_in.shape[0]
    half = low_rank // 2
    tokens = act_ref.shape[0]
    for copy in scalars:
        copy.wait()
    mine = jnp.int32(-1)
    for query in reversed(range(owners.shape[0])):
        hit = owners[query] == me
        if slot:
            hit = hit & (rank_of(owners, query) == slot)
        mine = jnp.where(hit, steps[query], mine)

    def tell_sharing():
        sharing = jnp.int32(0)
        for query in range(owners.shape[0]):
            on_line = line_rank(owners, query)
            twins = rank_of(owners, query)
            sharing = jnp.maximum(sharing, jnp.where(twins > 0, TWINS, on_line))
        sharing_ref[0] = sharing

    @pl.when(mine < 0)
    def _():
        out_ref[...] = jnp.zeros_like(out_ref)
        tell_sharing()
        for copy in weights:
            copy.wait()

    @pl.when(mine >= 0)
    def _():
        begin = jnp.int32(0)
        for step in range(lengths.shape[1]):
            begin = begin + jnp.where(step < mine, lengths[0, step], 0)
        end = begin + lengths[0, mine]

        def finish(size):
            first = jnp.minimum(lax.shift_right_logical(begin, bits(ALIGN)), (tokens - size) // ALIGN)
            first = pl.multiple_of(first * ALIGN, ALIGN)
            rows = [
                pltpu.make_async_copy(
                    source.at[pl.ds(first, size)], held.at[pl.ds(0, size)], row_sems.at[which]
                )
                for which, (source, held) in enumerate(((act_ref, act_rows), (grad_ref, grad_rows)))
            ]
            for copy in rows:
                copy.start()
            tell_sharing()
            position = first + lax.broadcasted_iota(jnp.int32, (size, low_rank), 0)
            inside = (position >= begin) & (position < end)
            for copy in weights + rows:
                copy.wait()
            lows = []
            for held, held_weights in ((act_rows, proj_in), (grad_rows, proj_out)):
                low = lax.dot_general(
                    held[:size], held_weights[...], NT, preferred_element_type=jnp.float32
                )
                lows.append(jnp.where(inside, low, 0.0).astype(jnp.bfloat16))
            step_grad = lax.dot_general(lows[0], lows[1], TN, preferred_element_type=jnp.float32)
            step_grad = step_grad.astype(jnp.bfloat16).astype(jnp.float32)
            right = lax.dot_general(
                step_grad, precond_out[...], NT, precision=HIGHEST, preferred_element_type=jnp.float32
            )
            both = lax.dot_general(
                precond_in[...], right, TN, precision=HIGHEST, preferred_element_type=jnp.float32
            )
            packed = jnp.concatenate([both[:half], both[half:]], axis=1).astype(jnp.bfloat16)
            out_ref[...] = jnp.broadcast_to(packed[None], out_ref.shape)

        first_of_small = jnp.minimum(
            lax.shift_right_logical(begin, bits(ALIGN)), (tokens - SMALL) // ALIGN
        )
        small = end - first_of_small * ALIGN <= SMALL

        @pl.when(small)
        def _():
            finish(SMALL)

        @pl.when(jnp.logical_not(small))
        def _():
            finish(WINDOW)


def flagged(slot, peers, owner, step, lengths, act, grad, proj_in, proj_out, pre_out, pre_in):
    low_rank = proj_in.shape[0]
    return pl.pallas_call(
        functools.partial(flagged_kernel, slot),
        out_shape=(
            jax.ShapeDtypeStruct((peers, low_rank // 2, 2 * low_rank), jnp.bfloat16),
            jax.ShapeDtypeStruct((1,), jnp.int32),
        ),
        in_specs=[HBM] * 9,
        out_specs=(VMEM, SMEM),
        scratch_shapes=[
            pltpu.SMEM(owner.shape, jnp.int32),
            pltpu.SMEM(step.shape, jnp.int32),
            pltpu.SMEM(lengths.shape, jnp.int32),
            pltpu.VMEM((WINDOW, act.shape[1]), jnp.bfloat16),
            pltpu.VMEM((WINDOW, grad.shape[1]), jnp.bfloat16),
            pltpu.VMEM(proj_in.shape, jnp.bfloat16),
            pltpu.VMEM(proj_out.shape, jnp.bfloat16),
            pltpu.VMEM(pre_out.shape, jnp.float32),
            pltpu.VMEM(pre_in.shape, jnp.float32),
            pltpu.SemaphoreType.DMA((7,)),
            pltpu.SemaphoreType.DMA((2,)),
        ],
        compiler_params=pltpu.CompilerParams(vmem_limit_bytes=8 << 20),
    )(owner, step, lengths, act, grad, proj_in, proj_out, pre_out, pre_in)


def turned_dot(rows_ref, proj_ref):
    low = lax.dot_general(rows_ref[...], proj_ref[...], NT, preferred_element_type=jnp.float32)
    return low.astype(jnp.bfloat16).astype(jnp.float32).T.astype(jnp.bfloat16)


def project_act_kernel(rows_ref, proj_ref, low_ref):
    low_ref[...] = turned_dot(rows_ref, proj_ref)


def project_grad_kernel(rows_ref, proj_ref, lengths_ref, low_ref, member_ref):
    steps, tokens = member_ref.shape
    token_of = lax.broadcasted_iota(jnp.int32, (steps, tokens), 1) + pl.program_id(0) * tokens
    one = lax.broadcasted_iota(jnp.int32, (steps, steps), 0)
    other = lax.broadcasted_iota(jnp.int32, (steps, steps), 1)
    spread = jnp.broadcast_to(lengths_ref[...], (steps, steps))
    begins = jnp.sum(jnp.where(other < one, spread, 0), axis=1, keepdims=True)
    ends = jnp.sum(jnp.where(other <= one, spread, 0), axis=1, keepdims=True)
    member_ref[...] = ((token_of >= begins) & (token_of < ends)).astype(jnp.bfloat16)
    low_ref[...] = turned_dot(rows_ref, proj_ref)


def project(rows, proj, lengths=None):
    tokens, low_rank = rows.shape[0], proj.shape[0]
    block = tokens // BLOCKS
    low = jax.ShapeDtypeStruct((low_rank, tokens), jnp.bfloat16)
    low_spec = pl.BlockSpec((low_rank, block), lambda i: (0, i))
    rows_spec = pl.BlockSpec((block, rows.shape[1]), lambda i: (i, 0))
    options = dict(
        grid=(BLOCKS,),
        compiler_params=pltpu.CompilerParams(vmem_limit_bytes=8 << 20),
        cost_estimate=pl.CostEstimate(
            flops=2 * low_rank * rows.size, bytes_accessed=2 * rows.size, transcendentals=0
        ),
    )
    if lengths is None:
        return pl.pallas_call(
            project_act_kernel,
            out_shape=low,
            in_specs=[rows_spec, VMEM],
            out_specs=low_spec,
            **options,
        )(rows, proj)
    steps = lengths.shape[1]
    return pl.pallas_call(
        project_grad_kernel,
        out_shape=(low, jax.ShapeDtypeStruct((steps, tokens), jnp.bfloat16)),
        in_specs=[rows_spec, VMEM, VMEM],
        out_specs=(low_spec, pl.BlockSpec((steps, block), lambda i: (0, i))),
        **options,
    )(rows, proj, lengths)


def relay_one_kernel(received_ref, out_ref):
    only = jnp.sum(received_ref[...].astype(jnp.float32), axis=0).astype(jnp.bfloat16)
    out_ref[...] = jnp.broadcast_to(only[None], out_ref.shape)


def relay_one(peers, received):
    return pl.pallas_call(
        relay_one_kernel,
        out_shape=jax.ShapeDtypeStruct((peers,) + received.shape[1:], received.dtype),
        in_specs=[VMEM],
        out_specs=VMEM,
        compiler_params=pltpu.CompilerParams(vmem_limit_bytes=4 << 20),
    )(received)


def relay_two_kernel(owner_ref, received_ref, out_ref):
    here = plane_of(lax.axis_index(DP))
    for slot in range(out_ref.shape[1]):
        source = jnp.int32(0)
        for query in range(owner_ref.shape[0]):
            hit = (plane_of(owner_ref[query]) == here) & (line_rank(owner_ref, query) == slot)
            source = jnp.where(hit, line_of(owner_ref[query]), source)
        value = received_ref[source]
        out_ref[:, slot] = jnp.broadcast_to(value[None], out_ref[:, slot].shape)


def relay_two(peers, owner, received):
    return pl.pallas_call(
        relay_two_kernel,
        out_shape=jax.ShapeDtypeStruct((peers, 2) + received.shape[1:], received.dtype),
        in_specs=[SMEM, VMEM],
        out_specs=VMEM,
        compiler_params=pltpu.CompilerParams(vmem_limit_bytes=4 << 20),
    )(owner, received)


def relay_kernel(owner_ref, received_ref, more_ref, out_ref):
    for query in range(owner_ref.shape[0]):
        first = received_ref[line_of(owner_ref[query])]
        value = jnp.where(rank_of(owner_ref, query) == 0, first, more_ref[query])
        out_ref[:, query] = jnp.broadcast_to(value[None], out_ref[:, query].shape)


def relay(peers, owner, received, more):
    return pl.pallas_call(
        relay_kernel,
        out_shape=jax.ShapeDtypeStruct((peers,) + more.shape, more.dtype),
        in_specs=[SMEM, VMEM, VMEM],
        out_specs=VMEM,
        compiler_params=pltpu.CompilerParams(vmem_limit_bytes=4 << 20),
    )(owner, received, more)


def score_kernel(owner_ref, act_ref, grad_ref, member_ref, received_ref, out_ref):
    count = owner_ref.shape[0]
    low_rank, tokens = act_ref.shape
    steps = member_ref.shape[0]
    held = []
    for query in range(count):
        place = plane_of(owner_ref[query])
        if len(received_ref.shape) == 3:
            packed = received_ref[place]
        elif received_ref.shape[1] == count:
            packed = received_ref[place, query]
        else:
            packed = received_ref[place, line_rank(owner_ref, query)]
        held += [packed[:, :low_rank], packed[:, low_rank:]]
    weighted = jnp.concatenate(held, axis=0)
    turned = jnp.dot(weighted, grad_ref[...], preferred_element_type=jnp.float32)
    act_low = act_ref[...].astype(jnp.float32)
    value = turned.reshape(count, low_rank, tokens) * act_low[None]
    value = value.reshape(count * low_rank, tokens)
    high = value.astype(jnp.bfloat16)
    low = (value - high.astype(jnp.float32)).astype(jnp.bfloat16)
    member = member_ref[...]
    summed = lax.dot_general(
        high, member, NT, preferred_element_type=jnp.float32
    ) + lax.dot_general(low, member, NT, preferred_element_type=jnp.float32)
    table = jnp.sum(summed.reshape(count, low_rank, steps), axis=1)
    row = jnp.concatenate([table[query : query + 1] for query in range(count)], axis=1)
    out_ref[...] = jnp.broadcast_to(row, out_ref.shape)


def score(peers, owner, act_low, grad_low, member, received):
    count, steps = owner.shape[0], member.shape[0]
    return pl.pallas_call(
        score_kernel,
        out_shape=jax.ShapeDtypeStruct((peers, count * steps), jnp.float32),
        in_specs=[SMEM, VMEM, VMEM, VMEM, VMEM],
        out_specs=VMEM,
        compiler_params=pltpu.CompilerParams(vmem_limit_bytes=8 << 20),
    )(owner, act_low, grad_low, member, received)


def pick_kernel(layers, scale, retrieval_ref, table_ref, out_ref):
    count, per_scorer = retrieval_ref.shape
    rows, width = table_ref.shape
    steps = width // count
    shift = steps.bit_length() - 1
    ids = retrieval_ref[...]
    wanted = jnp.concatenate([ids[query : query + 1] for query in range(count)], axis=1)
    total = wanted.shape[1]
    source = lax.shift_right_logical(wanted, shift)
    first = lax.broadcasted_iota(jnp.int32, (1, total), 1) // per_scorer * steps
    entry = lax.bitwise_and(wanted, steps - 1) + first
    table_row = lax.broadcasted_iota(jnp.int32, (rows, total), 0) // layers
    chosen = jnp.where(table_row == source, 1.0, 0.0).astype(jnp.bfloat16)
    rest = table_ref[...]
    values = jnp.zeros((width, total), jnp.float32)
    for _ in range(3):
        piece = rest.astype(jnp.bfloat16)
        values = values + lax.dot_general(piece, chosen, TN, preferred_element_type=jnp.float32)
        rest = rest - piece.astype(jnp.float32)
    entry_row = lax.broadcasted_iota(jnp.int32, (width, total), 0)
    found = scale * jnp.sum(jnp.where(entry_row == entry, values, 0.0), axis=0, keepdims=True)
    for query in range(count):
        out_ref[query : query + 1] = found[:, query * per_scorer : (query + 1) * per_scorer]


def pick(layers, scale, retrieval, table):
    return pl.pallas_call(
        functools.partial(pick_kernel, layers, scale),
        out_shape=jax.ShapeDtypeStruct(retrieval.shape, jnp.float32),
        in_specs=[VMEM, VMEM],
        out_specs=VMEM,
        compiler_params=pltpu.CompilerParams(vmem_limit_bytes=4 << 20),
    )(retrieval, table)


def local(
    activations,
    out_grads,
    proj_in,
    proj_out,
    precond_out,
    precond_in,
    step_lengths,
    flagged_owner,
    flagged_step,
    retrieval,
):
    low_rank = precond_in.shape[1]
    count = flagged_owner.shape[0]
    layers = lax.axis_size("layer")
    peers = lax.axis_size(DP + ("layer",))
    act, grad = activations[0], out_grads[0]
    into, outof = proj_in[0].T, proj_out[0].T

    def swap(value, axes):
        return lax.all_to_all(value, axes, split_axis=0, concat_axis=0, tiled=True)

    def own_slot(slot):
        return flagged(
            slot, SIZES[1], flagged_owner, flagged_step, step_lengths,
            act, grad, into, outof, precond_out[0], precond_in[0],
        )

    def further_slots():
        earlier = jnp.arange(count)[None, :] < jnp.arange(count)[:, None]
        same = flagged_owner[:, None] == flagged_owner[None, :]
        ranks = jnp.sum((earlier & same).astype(jnp.int32), axis=1)
        slots = jnp.stack([own_slot(slot)[0] for slot in range(1, count)], axis=1)
        return swap(slots, "z")[line_of(flagged_owner), jnp.maximum(ranks - 1, 0)]

    def no_further():
        return jnp.zeros((count, low_rank // 2, 2 * low_rank), jnp.bfloat16)

    def scored(plane, cols):
        in_plane = swap(plane, PLANE)
        grad_low, member = project(cols, outof, step_lengths)
        in_plane, grad_low, member = lax.optimization_barrier((in_plane, grad_low, member))
        return score(peers, flagged_owner, act_low, grad_low, member, in_plane)

    def one_a_line(in_line, cols):
        return scored(relay_one(width, in_line), cols)

    def two_a_line(in_line, cols):
        return scored(relay_two(width, flagged_owner, in_line), cols)

    def any_owners(in_line, cols):
        more = lax.cond(sharing[0] >= TWINS, further_slots, no_further)
        return scored(relay(width, flagged_owner, in_line, more), cols)

    width = SIZES[0] * SIZES[2]
    own, sharing = own_slot(0)
    in_line = swap(own, "z")
    act_low = project(act, into)
    sharing, act_low = lax.optimization_barrier((sharing, act_low))
    path = jnp.minimum(sharing[0], 2)
    in_line, path, act_low, cols = lax.optimization_barrier((in_line, path, act_low, grad))
    table = lax.switch(path, (one_a_line, two_a_line, any_owners), in_line, cols)
    tables = swap(table, DP + ("layer",))
    return pick(layers, 1.0 / (low_rank * STEP_MAX), retrieval, tables)


def solution(mesh):
    parts = Mesh(mesh.devices.reshape(SIZES + (mesh.shape["layer"],)), DP + ("layer",))
    return jax.shard_map(
        local,
        mesh=parts,
        in_specs=(
            P("layer", DP, None),
            P("layer", DP, None),
            P("layer", None, None),
            P("layer", None, None),
            P("layer", None, None),
            P("layer", None, None),
            P(DP, None),
            P(),
            P(),
            P(None, DP),
        ),
        out_specs=P(None, DP),
        check_vma=False,
    )
```

```python
import functools

import jax
import jax.numpy as jnp
from jax import lax
from jax.experimental import pallas as pl
from jax.experimental.pallas import tpu as pltpu
from jax.sharding import Mesh, PartitionSpec as P

WINDOW = 80
SMALL = 32
TWINS = 4
ALIGN = 16
BLOCKS = 2
STEP_MAX = 64
SIZES = (4, 8, 4)
DP = ("y", "z", "x")
PLANE = ("y", "x")
NT = (((1,), (1,)), ((), ()))
TN = (((0,), (0,)), ((), ()))
HIGHEST = lax.Precision.HIGHEST
SMEM = pl.BlockSpec(memory_space=pltpu.SMEM)
VMEM = pl.BlockSpec(memory_space=pltpu.VMEM)
HBM = pl.BlockSpec(memory_space=pl.ANY)


def rank_of(owner_ref, query):
    rank = jnp.int32(0)
    for other in range(query):
        rank = rank + jnp.where(owner_ref[other] == owner_ref[query], 1, 0).astype(jnp.int32)
    return rank


def bits(size):
    return size.bit_length() - 1


def line_of(owner):
    return lax.bitwise_and(lax.shift_right_logical(owner, bits(SIZES[2])), SIZES[1] - 1)


def plane_of(owner):
    row = lax.shift_right_logical(owner, bits(SIZES[1] * SIZES[2]))
    return row * SIZES[2] + lax.bitwise_and(owner, SIZES[2] - 1)


def line_rank(owner_ref, query):
    rank = jnp.int32(0)
    for other in range(query):
        shared = plane_of(owner_ref[other]) == plane_of(owner_ref[query])
        rank = rank + jnp.where(shared, 1, 0).astype(jnp.int32)
    return rank


def flagged_kernel(
    slot,
    owner_ref,
    step_ref,
    lengths_ref,
    act_ref,
    grad_ref,
    proj_in_ref,
    proj_out_ref,
    precond_out_ref,
    precond_in_ref,
    out_ref,
    sharing_ref,
    owners,
    steps,
    lengths,
    act_rows,
    grad_rows,
    proj_in,
    proj_out,
    precond_out,
    precond_in,
    sems,
    row_sems,
):
    scalars = [
        pltpu.make_async_copy(source, held, sems.at[i])
        for i, (source, held) in enumerate(
            ((owner_ref, owners), (step_ref, steps), (lengths_ref, lengths))
        )
    ]
    weights = [
        pltpu.make_async_copy(source, held, sems.at[3 + i])
        for i, (source, held) in enumerate(
            (
                (proj_in_ref, proj_in),
                (proj_out_ref, proj_out),
                (precond_out_ref, precond_out),
                (precond_in_ref, precond_in),
            )
        )
    ]
    for copy in scalars + weights:
        copy.start()
    me = lax.axis_index(DP)
    low_rank = proj_in.shape[0]
    half = low_rank // 2
    tokens = act_ref.shape[0]
    for copy in scalars:
        copy.wait()
    mine = jnp.int32(-1)
    for query in reversed(range(owners.shape[0])):
        hit = owners[query] == me
        if slot:
            hit = hit & (rank_of(owners, query) == slot)
        mine = jnp.where(hit, steps[query], mine)

    def tell_sharing():
        sharing = jnp.int32(0)
        for query in range(owners.shape[0]):
            on_line = line_rank(owners, query)
            twins = rank_of(owners, query)
            sharing = jnp.maximum(sharing, jnp.where(twins > 0, TWINS, on_line))
        sharing_ref[0] = sharing

    @pl.when(mine < 0)
    def _():
        out_ref[...] = jnp.zeros_like(out_ref)
        tell_sharing()
        for copy in weights:
            copy.wait()

    @pl.when(mine >= 0)
    def _():
        begin = jnp.int32(0)
        for step in range(lengths.shape[1]):
            begin = begin + jnp.where(step < mine, lengths[0, step], 0)
        end = begin + lengths[0, mine]

        def finish(size):
            first = jnp.minimum(lax.shift_right_logical(begin, bits(ALIGN)), (tokens - size) // ALIGN)
            first = pl.multiple_of(first * ALIGN, ALIGN)
            rows = [
                pltpu.make_async_copy(
                    source.at[pl.ds(first, size)], held.at[pl.ds(0, size)], row_sems.at[which]
                )
                for which, (source, held) in enumerate(((act_ref, act_rows), (grad_ref, grad_rows)))
            ]
            for copy in rows:
                copy.start()
            tell_sharing()
            position = first + lax.broadcasted_iota(jnp.int32, (size, low_rank), 0)
            inside = (position >= begin) & (position < end)
            for copy in weights + rows:
                copy.wait()
            lows = []
            for held, held_weights in ((act_rows, proj_in), (grad_rows, proj_out)):
                low = lax.dot_general(
                    held[:size], held_weights[...], NT, preferred_element_type=jnp.float32
                )
                lows.append(jnp.where(inside, low, 0.0).astype(jnp.bfloat16))
            step_grad = lax.dot_general(lows[0], lows[1], TN, preferred_element_type=jnp.float32)
            step_grad = step_grad.astype(jnp.bfloat16).astype(jnp.float32)
            right = lax.dot_general(
                step_grad, precond_out[...], NT, precision=HIGHEST, preferred_element_type=jnp.float32
            )
            both = lax.dot_general(
                precond_in[...], right, TN, precision=HIGHEST, preferred_element_type=jnp.float32
            )
            packed = jnp.concatenate([both[:half], both[half:]], axis=1).astype(jnp.bfloat16)
            out_ref[...] = jnp.broadcast_to(packed[None], out_ref.shape)

        first_of_small = jnp.minimum(
            lax.shift_right_logical(begin, bits(ALIGN)), (tokens - SMALL) // ALIGN
        )
        small = end - first_of_small * ALIGN <= SMALL

        @pl.when(small)
        def _():
            finish(SMALL)

        @pl.when(jnp.logical_not(small))
        def _():
            finish(WINDOW)


def flagged(slot, peers, owner, step, lengths, act, grad, proj_in, proj_out, pre_out, pre_in):
    low_rank = proj_in.shape[0]
    return pl.pallas_call(
        functools.partial(flagged_kernel, slot),
        out_shape=(
            jax.ShapeDtypeStruct((peers, low_rank // 2, 2 * low_rank), jnp.bfloat16),
            jax.ShapeDtypeStruct((1,), jnp.int32),
        ),
        in_specs=[HBM] * 9,
        out_specs=(VMEM, SMEM),
        scratch_shapes=[
            pltpu.SMEM(owner.shape, jnp.int32),
            pltpu.SMEM(step.shape, jnp.int32),
            pltpu.SMEM(lengths.shape, jnp.int32),
            pltpu.VMEM((WINDOW, act.shape[1]), jnp.bfloat16),
            pltpu.VMEM((WINDOW, grad.shape[1]), jnp.bfloat16),
            pltpu.VMEM(proj_in.shape, jnp.bfloat16),
            pltpu.VMEM(proj_out.shape, jnp.bfloat16),
            pltpu.VMEM(pre_out.shape, jnp.float32),
            pltpu.VMEM(pre_in.shape, jnp.float32),
            pltpu.SemaphoreType.DMA((7,)),
            pltpu.SemaphoreType.DMA((2,)),
        ],
        compiler_params=pltpu.CompilerParams(vmem_limit_bytes=8 << 20),
    )(owner, step, lengths, act, grad, proj_in, proj_out, pre_out, pre_in)


def turned_dot(rows_ref, proj_ref):
    low = lax.dot_general(rows_ref[...], proj_ref[...], NT, preferred_element_type=jnp.float32)
    return low.astype(jnp.bfloat16).astype(jnp.float32).T.astype(jnp.bfloat16)


def project_act_kernel(rows_ref, proj_ref, low_ref):
    low_ref[...] = turned_dot(rows_ref, proj_ref)


def project_grad_kernel(rows_ref, proj_ref, lengths_ref, low_ref, member_ref):
    steps, tokens = member_ref.shape
    token_of = lax.broadcasted_iota(jnp.int32, (steps, tokens), 1) + pl.program_id(0) * tokens
    one = lax.broadcasted_iota(jnp.int32, (steps, steps), 0)
    other = lax.broadcasted_iota(jnp.int32, (steps, steps), 1)
    spread = jnp.broadcast_to(lengths_ref[...], (steps, steps))
    begins = jnp.sum(jnp.where(other < one, spread, 0), axis=1, keepdims=True)
    ends = jnp.sum(jnp.where(other <= one, spread, 0), axis=1, keepdims=True)
    member_ref[...] = ((token_of >= begins) & (token_of < ends)).astype(jnp.bfloat16)
    low_ref[...] = turned_dot(rows_ref, proj_ref)


def project(rows, proj, lengths=None):
    tokens, low_rank = rows.shape[0], proj.shape[0]
    block = tokens // BLOCKS
    low = jax.ShapeDtypeStruct((low_rank, tokens), jnp.bfloat16)
    low_spec = pl.BlockSpec((low_rank, block), lambda i: (0, i))
    rows_spec = pl.BlockSpec((block, rows.shape[1]), lambda i: (i, 0))
    options = dict(
        grid=(BLOCKS,),
        compiler_params=pltpu.CompilerParams(vmem_limit_bytes=8 << 20),
        cost_estimate=pl.CostEstimate(
            flops=2 * low_rank * rows.size, bytes_accessed=2 * rows.size, transcendentals=0
        ),
    )
    if lengths is None:
        return pl.pallas_call(
            project_act_kernel,
            out_shape=low,
            in_specs=[rows_spec, VMEM],
            out_specs=low_spec,
            **options,
        )(rows, proj)
    steps = lengths.shape[1]
    return pl.pallas_call(
        project_grad_kernel,
        out_shape=(low, jax.ShapeDtypeStruct((steps, tokens), jnp.bfloat16)),
        in_specs=[rows_spec, VMEM, VMEM],
        out_specs=(low_spec, pl.BlockSpec((steps, block), lambda i: (0, i))),
        **options,
    )(rows, proj, lengths)


def relay_one_kernel(received_ref, out_ref):
    only = jnp.sum(received_ref[...].astype(jnp.float32), axis=0).astype(jnp.bfloat16)
    out_ref[...] = jnp.broadcast_to(only[None], out_ref.shape)


def relay_one(peers, received):
    return pl.pallas_call(
        relay_one_kernel,
        out_shape=jax.ShapeDtypeStruct((peers,) + received.shape[1:], received.dtype),
        in_specs=[VMEM],
        out_specs=VMEM,
        compiler_params=pltpu.CompilerParams(vmem_limit_bytes=4 << 20),
    )(received)


def relay_two_kernel(owner_ref, received_ref, out_ref):
    here = plane_of(lax.axis_index(DP))
    for slot in range(out_ref.shape[1]):
        source = jnp.int32(0)
        for query in range(owner_ref.shape[0]):
            hit = (plane_of(owner_ref[query]) == here) & (line_rank(owner_ref, query) == slot)
            source = jnp.where(hit, line_of(owner_ref[query]), source)
        value = received_ref[source]
        out_ref[:, slot] = jnp.broadcast_to(value[None], out_ref[:, slot].shape)


def relay_two(peers, owner, received):
    return pl.pallas_call(
        relay_two_kernel,
        out_shape=jax.ShapeDtypeStruct((peers, 2) + received.shape[1:], received.dtype),
        in_specs=[SMEM, VMEM],
        out_specs=VMEM,
        compiler_params=pltpu.CompilerParams(vmem_limit_bytes=4 << 20),
    )(owner, received)


def relay_kernel(owner_ref, received_ref, more_ref, out_ref):
    for query in range(owner_ref.shape[0]):
        first = received_ref[line_of(owner_ref[query])]
        value = jnp.where(rank_of(owner_ref, query) == 0, first, more_ref[query])
        out_ref[:, query] = jnp.broadcast_to(value[None], out_ref[:, query].shape)


def relay(peers, owner, received, more):
    return pl.pallas_call(
        relay_kernel,
        out_shape=jax.ShapeDtypeStruct((peers,) + more.shape, more.dtype),
        in_specs=[SMEM, VMEM, VMEM],
        out_specs=VMEM,
        compiler_params=pltpu.CompilerParams(vmem_limit_bytes=4 << 20),
    )(owner, received, more)


def score_kernel(owner_ref, act_ref, grad_ref, member_ref, received_ref, out_ref):
    count = owner_ref.shape[0]
    low_rank, tokens = act_ref.shape
    steps = member_ref.shape[0]
    held = []
    for query in range(count):
        place = plane_of(owner_ref[query])
        if len(received_ref.shape) == 3:
            packed = received_ref[place]
        elif received_ref.shape[1] == count:
            packed = received_ref[place, query]
        else:
            packed = received_ref[place, line_rank(owner_ref, query)]
        held += [packed[:, :low_rank], packed[:, low_rank:]]
    weighted = jnp.concatenate(held, axis=0)
    turned = jnp.dot(weighted, grad_ref[...], preferred_element_type=jnp.float32)
    act_low = act_ref[...].astype(jnp.float32)
    value = turned.reshape(count, low_rank, tokens) * act_low[None]
    value = value.reshape(count * low_rank, tokens)
    high = value.astype(jnp.bfloat16)
    low = (value - high.astype(jnp.float32)).astype(jnp.bfloat16)
    member = member_ref[...]
    summed = lax.dot_general(
        high, member, NT, preferred_element_type=jnp.float32
    ) + lax.dot_general(low, member, NT, preferred_element_type=jnp.float32)
    table = jnp.sum(summed.reshape(count, low_rank, steps), axis=1)
    row = jnp.concatenate([table[query : query + 1] for query in range(count)], axis=1)
    out_ref[...] = jnp.broadcast_to(row, out_ref.shape)


def score(peers, owner, act_low, grad_low, member, received):
    count, steps = owner.shape[0], member.shape[0]
    return pl.pallas_call(
        score_kernel,
        out_shape=jax.ShapeDtypeStruct((peers, count * steps), jnp.float32),
        in_specs=[SMEM, VMEM, VMEM, VMEM, VMEM],
        out_specs=VMEM,
        compiler_params=pltpu.CompilerParams(vmem_limit_bytes=8 << 20),
    )(owner, act_low, grad_low, member, received)


def combine_kernel(own_ref, other_ref, out_ref):
    out_ref[...] = jnp.broadcast_to(own_ref[...] + other_ref[...], out_ref.shape)


def combine(peers, own, other):
    return pl.pallas_call(
        combine_kernel,
        out_shape=jax.ShapeDtypeStruct((peers, own.shape[1]), own.dtype),
        in_specs=[VMEM, VMEM],
        out_specs=VMEM,
        compiler_params=pltpu.CompilerParams(vmem_limit_bytes=4 << 20),
    )(own, other)


def pick_kernel(layers, scale, retrieval_ref, table_ref, out_ref):
    count, per_scorer = retrieval_ref.shape
    rows, width = table_ref.shape
    steps = width // count
    shift = steps.bit_length() - 1
    ids = retrieval_ref[...]
    wanted = jnp.concatenate([ids[query : query + 1] for query in range(count)], axis=1)
    total = wanted.shape[1]
    source = lax.shift_right_logical(wanted, shift)
    first = lax.broadcasted_iota(jnp.int32, (1, total), 1) // per_scorer * steps
    entry = lax.bitwise_and(wanted, steps - 1) + first
    table_row = lax.broadcasted_iota(jnp.int32, (rows, total), 0) // layers
    chosen = jnp.where(table_row == source, 1.0, 0.0).astype(jnp.bfloat16)
    rest = table_ref[...]
    values = jnp.zeros((width, total), jnp.float32)
    for _ in range(3):
        piece = rest.astype(jnp.bfloat16)
        values = values + lax.dot_general(piece, chosen, TN, preferred_element_type=jnp.float32)
        rest = rest - piece.astype(jnp.float32)
    entry_row = lax.broadcasted_iota(jnp.int32, (width, total), 0)
    found = scale * jnp.sum(jnp.where(entry_row == entry, values, 0.0), axis=0, keepdims=True)
    for query in range(count):
        out_ref[query : query + 1] = found[:, query * per_scorer : (query + 1) * per_scorer]


def pick(layers, scale, retrieval, table):
    return pl.pallas_call(
        functools.partial(pick_kernel, layers, scale),
        out_shape=jax.ShapeDtypeStruct(retrieval.shape, jnp.float32),
        in_specs=[VMEM, VMEM],
        out_specs=VMEM,
        compiler_params=pltpu.CompilerParams(vmem_limit_bytes=4 << 20),
    )(retrieval, table)


def local(
    activations,
    out_grads,
    proj_in,
    proj_out,
    precond_out,
    precond_in,
    step_lengths,
    flagged_owner,
    flagged_step,
    retrieval,
):
    low_rank = precond_in.shape[1]
    count = flagged_owner.shape[0]
    layers = lax.axis_size("layer")
    peers = lax.axis_size(DP)
    act, grad = activations[0], out_grads[0]
    into, outof = proj_in[0].T, proj_out[0].T

    def swap(value, axes):
        return lax.all_to_all(value, axes, split_axis=0, concat_axis=0, tiled=True)

    def own_slot(slot):
        return flagged(
            slot, SIZES[1], flagged_owner, flagged_step, step_lengths,
            act, grad, into, outof, precond_out[0], precond_in[0],
        )

    def further_slots():
        earlier = jnp.arange(count)[None, :] < jnp.arange(count)[:, None]
        same = flagged_owner[:, None] == flagged_owner[None, :]
        ranks = jnp.sum((earlier & same).astype(jnp.int32), axis=1)
        slots = jnp.stack([own_slot(slot)[0] for slot in range(1, count)], axis=1)
        return swap(slots, "z")[line_of(flagged_owner), jnp.maximum(ranks - 1, 0)]

    def no_further():
        return jnp.zeros((count, low_rank // 2, 2 * low_rank), jnp.bfloat16)

    def scored(plane, cols):
        in_plane = swap(plane, PLANE)
        grad_low, member = project(cols, outof, step_lengths)
        in_plane, grad_low, member = lax.optimization_barrier((in_plane, grad_low, member))
        return score(1, flagged_owner, act_low, grad_low, member, in_plane)

    def one_a_line(in_line, cols):
        return scored(relay_one(width, in_line), cols)

    def two_a_line(in_line, cols):
        return scored(relay_two(width, flagged_owner, in_line), cols)

    def any_owners(in_line, cols):
        more = lax.cond(sharing[0] >= TWINS, further_slots, no_further)
        return scored(relay(width, flagged_owner, in_line, more), cols)

    width = SIZES[0] * SIZES[2]
    own, sharing = own_slot(0)
    in_line = swap(own, "z")
    act_low = project(act, into)
    sharing, act_low = lax.optimization_barrier((sharing, act_low))
    path = jnp.minimum(sharing[0], 2)
    in_line, path, act_low, cols = lax.optimization_barrier((in_line, path, act_low, grad))
    table = lax.switch(path, (one_a_line, two_a_line, any_owners), in_line, cols)
    other = lax.ppermute(table, "layer", [(i, layers - 1 - i) for i in range(layers)])
    tables = swap(combine(peers, table, other), DP)
    return pick(1, 1.0 / (low_rank * STEP_MAX), retrieval, tables)


def solution(mesh):
    parts = Mesh(mesh.devices.reshape(SIZES + (mesh.shape["layer"],)), DP + ("layer",))
    return jax.shard_map(
        local,
        mesh=parts,
        in_specs=(
            P("layer", DP, None),
            P("layer", DP, None),
            P("layer", None, None),
            P("layer", None, None),
            P("layer", None, None),
            P("layer", None, None),
            P(DP, None),
            P(),
            P(),
            P(None, DP),
        ),
        out_specs=P(None, DP),
        check_vma=False,
    )
```
